128 devices in a mesh: section: 2 (over z_lo), ctx: 32 (over y, x, core), wsh: 2 (over z_hi).
Axes of the slice: x: 4, y: 4, z: 4 (z_hi: 2, z_lo: 2; z = z_hi * 2 + z_lo), core: 2. Of those that a mesh axis runs over, the one named last changes fastest.
Arguments:
- inputs: bfloat16 [2, 2, 4096, 576], P(None, 'wsh', 'ctx'), may hold values from -6 to 6
- cotangent: bfloat16 [2, 2, 4096, 576], P(None, 'wsh', 'ctx'), may hold values from -6 to 6
- positions: int32 [2, 2, 4096], P(None, 'wsh', 'ctx'), may hold values from 0 to 4095, as said below
- norm_attn: bfloat16 [2, 576], P('section', 'wsh'), may hold values from 0.5 to 1.5
- w_query: bfloat16 [2, 576, 576], P('section', 'wsh'), may hold values from -0.25 to 0.25
- w_key: bfloat16 [2, 576, 192], P('section', 'wsh'), may hold values from -0.25 to 0.25
- w_value: bfloat16 [2, 576, 192], P('section', 'wsh'), may hold values from -0.25 to 0.25
- w_out: bfloat16 [2, 576, 576], P('section', 'wsh'), may hold values from -2 to 2
- norm_mlp: bfloat16 [2, 576], P('section', 'wsh'), may hold values from 0.5 to 1.5
- w_gate: bfloat16 [2, 576, 1536], P('section', 'wsh'), may hold values from -0.25 to 0.25
- w_up: bfloat16 [2, 576, 1536], P('section', 'wsh'), may hold values from -0.25 to 0.25
- w_down: bfloat16 [2, 1536, 576], P('section', 'wsh'), may hold values from -0.15625 to 0.15625
Outputs:
- activations: bfloat16 [2, 2, 2, 4096, 576], P('section', None, 'wsh', 'ctx')
- input_grads: float32 [2, 2, 2, 4096, 576], P('section', None, 'wsh', 'ctx')
- grad_norm_attn: float32 [2, 576], P('section', 'wsh')
- grad_query: float32 [2, 576, 576], P('section', 'wsh')
- grad_key: float32 [2, 576, 192], P('section', 'wsh')
- grad_value: float32 [2, 576, 192], P('section', 'wsh')
- grad_out: float32 [2, 576, 576], P('section', 'wsh')
- grad_norm_mlp: float32 [2, 576], P('section', 'wsh')
- grad_gate: float32 [2, 576, 1536], P('section', 'wsh')
- grad_up: float32 [2, 576, 1536], P('section', 'wsh')
- grad_down: float32 [2, 1536, 576], P('section', 'wsh')
The draws below stay inside these ranges and needn't reach their ends.
Inputs may be any that keep to these rules, and one draw needn't show every extreme that they name: `positions`: for each micro-batch and sequence the 4096 entries are a permutation of 0 to 4095 made of runs of 64 consecutive numbers, each run starting at a multiple of 64.
All inputs are finite; a program needn't handle non-finite values.
Results may differ from the reference program's by a relative error of at most 0.029.
Values may be sent and summed in bfloat16 or wider, within the bound.
No kernel may reach another device: no remote copies, remote signals or barrier semaphores. Data moves between devices by JAX's collectives and lax.ppermute only.
A program may use at most 128 MiB of HBM per device.

```python
import jax
import jax.numpy as jnp
from jax import lax

D = 576
FF = 1536
HEADS = 9
KV_HEADS = 3
HEAD_DIM = 64
SPAN = 128
MB = 2
SECTIONS = 2
SEQS = 2
L = 4096


def draw_positions(key, part):
    key = jax.random.fold_in(key, 11)
    half = SPAN // 2
    blocks = L // half
    keys = jax.random.split(key, MB * SEQS)
    order = jax.vmap(lambda single: jax.random.permutation(single, blocks))(keys)
    places = order[:, :, None] * half + jnp.arange(half, dtype=jnp.int32)[None, None, :]
    return places.reshape(MB, SEQS, L).astype(jnp.int32)


def block_levels(own_key, shape, shards, least, high):
    level = 1.0
    for position, blocks in shards:
        steps = jax.random.uniform(jax.random.fold_in(jax.random.fold_in(own_key, 6), position), (blocks,), jnp.float32, least / len(shards), high / len(shards))
        level = level * jnp.repeat(jnp.exp(steps), shape[position] // blocks).reshape((-1,) + (1,) * (len(shape) - 1 - position))
    return level


def scatter_about(rng, extent, spread, reach, pieces=(), kind=jnp.bfloat16):
    array = spread * jax.random.normal(rng, extent, jnp.float32)
    if pieces:
        array = array * block_levels(rng, extent, pieces, -0.22, 0.18)
    return jnp.clip(array, -reach, reach).astype(kind)


def setup_inputs(seed: int = 0) -> dict:
    streams_of = jax.random.split(jax.random.key(seed), 13)
    inputs = scatter_about(streams_of[0], (MB, SEQS, L, D), 1.0, 6.0, ((1, 2), (2, 32)))
    cotangent = scatter_about(streams_of[1], (MB, SEQS, L, D), 1.0, 6.0, ((1, 2), (2, 32)))
    positions = draw_positions(jax.random.fold_in(streams_of[12], 71), 0)
    norm_attn = jnp.clip(1.0 + 0.1 * jax.random.normal(streams_of[3], (SECTIONS, D), jnp.float32), 0.5, 1.5).astype(jnp.bfloat16)
    w_query = scatter_about(streams_of[4], (SECTIONS, D, HEADS * HEAD_DIM), D ** -0.5, 0.25, ((0, 2), (1, 2)))
    w_key = scatter_about(streams_of[5], (SECTIONS, D, KV_HEADS * HEAD_DIM), D ** -0.5, 0.25, ((0, 2), (1, 2)))
    w_value = scatter_about(streams_of[6], (SECTIONS, D, KV_HEADS * HEAD_DIM), D ** -0.5, 0.25, ((0, 2), (1, 2)))
    w_out = scatter_about(streams_of[7], (SECTIONS, HEADS * HEAD_DIM, D), (max(HEADS * HEAD_DIM // 64, 1)) ** -0.5, 2.0, ((0, 2), (1, 2)))
    norm_mlp = jnp.clip(1.0 + 0.1 * jax.random.normal(streams_of[8], (SECTIONS, D), jnp.float32), 0.5, 1.5).astype(jnp.bfloat16)
    w_gate = scatter_about(streams_of[9], (SECTIONS, D, FF), D ** -0.5, 0.25, ((0, 2), (1, 2)))
    w_up = scatter_about(streams_of[10], (SECTIONS, D, FF), D ** -0.5, 0.25, ((0, 2), (1, 2)))
    w_down = scatter_about(streams_of[11], (SECTIONS, FF, D), FF ** -0.5, 0.15625, ((0, 2), (1, 2)))
    return {"inputs": inputs, "cotangent": cotangent, "positions": positions, "norm_attn": norm_attn, "w_query": w_query, "w_key": w_key, "w_value": w_value, "w_out": w_out, "norm_mlp": norm_mlp, "w_gate": w_gate, "w_up": w_up, "w_down": w_down}


EPS = 1e-05
NEG = -1e+30
BASE = 100000.0

@jax.custom_vjp
def low(v):
    return lax.optimization_barrier(v.astype(jnp.bfloat16)).astype(jnp.float32)

@jax.custom_vjp
def low_back(v):
    return v

def low_keep(v):
    return (low(v), None)

def low_pass(kept, grad):
    return (grad,)

def back_keep(v):
    return (v, None)

def back_low(kept, grad):
    return (low(grad),)
low.defvjp(low_keep, low_pass)
low_back.defvjp(back_keep, back_low)

def multiply(left, right):
    return jnp.dot(left, right, precision=lax.Precision.HIGHEST)

def rope_tables(places, width):
    half = width // 2
    freq = BASE ** (-(jnp.arange(half, dtype=jnp.float32) * 2.0 / width))
    angle = places.astype(jnp.float32)[:, None] * freq[None, :]
    return (jnp.cos(angle), jnp.sin(angle))

def rotate(vector, cosine, sine):
    half = vector.shape[-1] // 2
    first = vector[..., :half]
    second = vector[..., half:]
    cosine = cosine[:, None, :]
    sine = sine[:, None, :]
    return jnp.concatenate([first * cosine - second * sine, second * cosine + first * sine], -1)

def layer(hidden, places, params):
    norm_attn, w_query, w_key, w_value, w_out, norm_mlp, w_gate, w_up, w_down = params
    length = hidden.shape[0]
    group = HEADS // KV_HEADS
    inverse = lax.rsqrt(lax.optimization_barrier(jnp.mean(hidden * hidden, -1, keepdims=True)) + EPS)
    rows_one = low(hidden * inverse * norm_attn)
    cosine, sine = rope_tables(places, HEAD_DIM)
    query = low(rotate(low_back(multiply(rows_one, w_query)).reshape(length, HEADS, HEAD_DIM), cosine, sine))
    query = query.reshape(length, KV_HEADS, group, HEAD_DIM)
    keys = low(rotate(low_back(multiply(rows_one, w_key)).reshape(length, KV_HEADS, HEAD_DIM), cosine, sine))
    values = low(low_back(multiply(rows_one, w_value))).reshape(length, KV_HEADS, HEAD_DIM)
    width_block = min(512, length)

    def attend_block(item):
        query_block, places_block = item
        scores = jnp.einsum('nkgd,mkd->kgnm', query_block, keys, precision=lax.Precision.HIGHEST)
        scores = low_back(scores * HEAD_DIM ** (-0.5))
        allowed = places[None, :] <= places_block[:, None]
        scores = jnp.where(allowed[None, None], scores, NEG)
        probs = low(jax.nn.softmax(scores, axis=-1))
        return jnp.einsum('kgnm,mkd->nkgd', probs, values, precision=lax.Precision.HIGHEST)
    mixed = lax.map(jax.checkpoint(attend_block), (query.reshape(length // width_block, width_block, KV_HEADS, group, HEAD_DIM), places.reshape(length // width_block, width_block)))
    mixed = low_back(low(mixed.reshape(length, HEADS * HEAD_DIM)))
    middle = hidden + low_back(multiply(mixed, w_out))
    inverse_two = lax.rsqrt(lax.optimization_barrier(jnp.mean(middle * middle, -1, keepdims=True)) + EPS)
    rows_two = low(middle * inverse_two * norm_mlp)
    gate = low_back(multiply(rows_two, w_gate))
    upper = low_back(multiply(rows_two, w_up))
    inner = low(jax.nn.silu(gate) * upper)
    return middle + low_back(multiply(inner, w_down))

def reference(inputs, cotangent, positions, norm_attn, w_query, w_key, w_value, w_out, norm_mlp, w_gate, w_up, w_down):
    count = MB * SEQS
    flat_inputs = inputs.astype(jnp.float32).reshape(count, L, D)
    flat_places = positions.reshape(count, L).astype(jnp.int32)
    params = tuple((item.astype(jnp.float32) for item in (norm_attn, w_query, w_key, w_value, w_out, norm_mlp, w_gate, w_up, w_down)))
    extra = jnp.zeros_like(flat_inputs)

    def forward(sources, added, *weights):

        def one(carry, item):
            sequence, addend, places = item
            first = layer(sequence, places, [w[0] for w in weights])
            lowered = low(first)
            second = layer(low_back(lowered) + addend, places, [w[1] for w in weights])
            return (carry, (second, lowered))
        _, (finals, middles) = lax.scan(one, jnp.zeros((), jnp.float32), (sources, added, flat_places))
        return (finals, middles)
    finals, pullback, middles = jax.vjp(forward, flat_inputs, extra, *params, has_aux=True)
    grads = pullback(cotangent.astype(jnp.float32).reshape(count, L, D))
    activations = jnp.stack([middles, finals]).reshape(2, MB, SEQS, L, D).astype(jnp.bfloat16)
    input_grads = jnp.stack([grads[0], grads[1]]).reshape(2, MB, SEQS, L, D)
    return (activations, input_grads, grads[2], grads[3], grads[4], grads[5], grads[6], grads[7], grads[8], grads[9], grads[10])
```

```python
import jax
import jax.numpy as jnp
from jax import lax
from jax.experimental import pallas as pl
from jax.experimental.pallas import tpu as pltpu
from jax.sharding import PartitionSpec as P

HEADS = 9
KV_HEADS = 3
GROUP = HEADS // KV_HEADS
HEAD_DIM = 64
D = HEADS * HEAD_DIM
FF = 1536
QKV = D + 2 * KV_HEADS * HEAD_DIM
KVW = 2 * KV_HEADS * HEAD_DIM
SPAN = 128
RUN = 64
LENGTH = 4096
RUNS = LENGTH // RUN
ROWS = GROUP * SPAN
BLOCK = 512
PIECES = LENGTH // BLOCK

EPS = 1e-05
NEG = -1e30
BASE = 100000.0
SCALE = HEAD_DIM ** (-0.5)

BF = jnp.bfloat16
F32 = jnp.float32
VMEM_LIMIT = 56 * 1024 * 1024


def nn(left, right):
    return lax.dot_general(left, right, (((1,), (0,)), ((), ())), preferred_element_type=F32)


def nt(left, right):
    return lax.dot_general(left, right, (((1,), (1,)), ((), ())), preferred_element_type=F32)


def normalize(hidden):
    inverse = lax.rsqrt(jnp.mean(hidden * hidden, -1, keepdims=True) + EPS)
    return hidden * inverse, inverse


def norm_back(grad, normed, inverse):
    return inverse * (grad - normed * jnp.mean(grad * normed, -1, keepdims=True))


def turn(head, cosine, sine):
    half = HEAD_DIM // 2
    first, second = head[:half], head[half:]
    return jnp.concatenate([first * cosine - second * sine, second * cosine + first * sine], 0)


def turn_back(head, cosine, sine):
    half = HEAD_DIM // 2
    first, second = head[:half], head[half:]
    return jnp.concatenate([first * cosine + second * sine, second * cosine - first * sine], 0)


def head_rows(array, head):
    return array[head * HEAD_DIM : (head + 1) * HEAD_DIM]


def group_of(array, group):
    return jnp.concatenate([head_rows(array, group * GROUP + r) for r in range(GROUP)], 1)


def ungroup(parts):
    return jnp.concatenate(
        [parts[g][:, r * SPAN : (r + 1) * SPAN] for g in range(KV_HEADS) for r in range(GROUP)], 0
    )


def attn_rows(hidden, gain):
    normed, inverse = normalize(hidden)
    return normed, inverse, (normed * gain).astype(BF)


def project(rows, w_qkv, cosine, sine, query_ref, kv_ref):
    flat = nn(rows, w_qkv).T
    heads = [turn(head_rows(flat, j), cosine, sine) * SCALE for j in range(HEADS)]
    for g in range(KV_HEADS):
        query_ref[g] = jnp.concatenate(heads[g * GROUP : (g + 1) * GROUP], 1).astype(BF)
    parts = []
    for g in range(KV_HEADS):
        parts.append(turn(head_rows(flat, HEADS + g), cosine, sine))
        parts.append(head_rows(flat, HEADS + KV_HEADS + g))
    kv_ref[...] = jnp.concatenate(parts, 0).T.astype(BF)


def one_hot(first_run, rows):
    lane = lax.broadcasted_iota(jnp.int32, (rows, SPAN), 1)
    run = lax.broadcasted_iota(jnp.int32, (rows, SPAN), 0) // RUN + first_run
    marked = (lane == run) | ((lane >= RUNS) & (lane < RUNS + 3))
    return jnp.where(marked, 1.0, 0.0).astype(BF)


def columns(g):
    return slice(g * SPAN, (g + 1) * SPAN)


def attend(query_ref, kv_refs, bias, triangle):
    zeros = jnp.zeros((HEAD_DIM, ROWS), BF)
    fixed = [jnp.concatenate([query_ref[g], zeros, bias, zeros], 0) for g in range(KV_HEADS)]
    triangle = jnp.concatenate([triangle] * GROUP, 1)
    start = []
    for g in range(KV_HEADS):
        own = kv_refs[0][:SPAN, columns(g)]
        scores = nn(own, fixed[g][:SPAN]) + triangle
        top = jnp.max(scores, 0, keepdims=True)
        probs = jnp.exp(scores - top)
        start += [top, jnp.sum(probs, 0, keepdims=True), nn(own.T[HEAD_DIM:], probs.astype(BF))]

    def step(b, carry):
        skip = SPAN if b == 0 else 0
        marks = one_hot((b * BLOCK + skip) // RUN, BLOCK - skip)
        out = []
        for g in range(KV_HEADS):
            top, total, accum = carry[3 * g : 3 * g + 3]
            block = kv_refs[b][skip:, columns(g)]
            scores = nn(jnp.concatenate([block, marks], 1), fixed[g])
            higher = jnp.maximum(top, jnp.max(scores, 0, keepdims=True))
            probs = jnp.exp(scores - higher)
            fade = jnp.exp(top - higher)
            total = total * fade + jnp.sum(probs, 0, keepdims=True)
            accum = accum * fade + nn(block.T[HEAD_DIM:], probs.astype(BF))
            out += [higher, total, accum]
        return tuple(out)

    done = tuple(start)
    for b in range(PIECES):
        done = step(b, done)
    mixed = [(done[3 * g + 2] / done[3 * g + 1]).astype(BF) for g in range(KV_HEADS)]
    logs = [done[3 * g] + jnp.log(done[3 * g + 1]) for g in range(KV_HEADS)]
    return mixed, logs


def attend_back(query_ref, kv_refs, bias, triangle, mixed, logs, mixed_grad, dkv_refs):
    zeros = jnp.zeros((HEAD_DIM, ROWS), BF)
    row = lax.broadcasted_iota(jnp.int32, (HEAD_DIM, 2 * ROWS), 0)
    triangle = jnp.concatenate([triangle] * GROUP, 1)
    fixed, turned = [], []
    for g in range(KV_HEADS):
        grads = group_of(mixed_grad, g)
        delta = jnp.sum(grads.astype(F32) * mixed[g].astype(F32), 0, keepdims=True)
        less = -jnp.concatenate([logs[g], delta], 1)
        high = less.astype(BF).astype(F32)
        middle = (less - high).astype(BF).astype(F32)
        lowest = less - high - middle
        stats = jnp.where(row == 0, high, jnp.where(row == 1, middle, jnp.where(row == 2, lowest, 0.0)))
        both = jnp.concatenate(
            [jnp.concatenate([query_ref[g], zeros], 1), jnp.concatenate([zeros, grads], 1)], 0
        )
        fixed.append(
            jnp.concatenate([both, jnp.concatenate([bias, zeros], 1), stats.astype(BF)], 0)
        )
        turned.append(both.T)

    def terms(block, marks, g, extra):
        both = nn(jnp.concatenate([block, marks], 1), fixed[g])
        scores = both[:, :ROWS]
        if extra is not None:
            scores = scores + extra
        probs = jnp.exp(scores)
        score_grad = (probs * both[:, ROWS:]).astype(BF)
        kv_terms = nn(jnp.concatenate([score_grad, probs.astype(BF)], 1), turned[g])
        return kv_terms.astype(BF), nn(block.T[:HEAD_DIM], score_grad)

    sums = [jnp.zeros((HEAD_DIM, ROWS), F32)] * KV_HEADS
    for b in range(PIECES):
        skip = SPAN if b == 0 else 0
        marks = one_hot((b * BLOCK + skip) // RUN, BLOCK - skip)
        for g in range(KV_HEADS):
            kv_terms, query_terms = terms(kv_refs[b][skip:, columns(g)], marks, g, None)
            dkv_refs[b][skip:, columns(g)] = kv_terms
            sums[g] = sums[g] + query_terms
    marks = one_hot(2 * RUNS, SPAN)
    for g in range(KV_HEADS):
        kv_terms, query_terms = terms(kv_refs[0][:SPAN, columns(g)], marks, g, triangle)
        dkv_refs[0][:SPAN, columns(g)] = kv_terms
        sums[g] = sums[g] + query_terms
    return ungroup(sums) * SCALE


def feed(middle, gain, w_gate, w_up):
    normed, inverse = normalize(middle)
    rows = (normed * gain).astype(BF)
    return normed, inverse, rows, nn(rows, w_gate), nn(rows, w_up)


def down(inner, w_down):
    half = FF // 2
    return nt(inner[:, :half], w_down[0]) + nt(inner[:, half:], w_down[1])


def feed_back(outgrad, middle, gain, w_gate, w_up, w_down, w_out, parts, refs):
    normed, inverse, rows, gate, upper = parts
    rows_ref, inner_ref, dgate_ref, dup_ref, df_ref, da_ref, gain_ref = refs
    sigma = jax.nn.sigmoid(gate)
    swish = gate * sigma
    df = outgrad.astype(BF)
    inner_grad = jnp.concatenate([nn(df, w_down[i]) for i in range(2)], 1)
    gate_grad = (inner_grad * upper * sigma * (1.0 + gate * (1.0 - sigma))).astype(BF)
    up_grad = (inner_grad * swish).astype(BF)
    rows_grad = nt(gate_grad, w_gate) + nt(up_grad, w_up)
    gain_ref[...] = jnp.sum(rows_grad * normed, 0, keepdims=True)
    middle_grad = outgrad + norm_back(rows_grad * gain, normed, inverse)
    da = middle_grad.astype(BF)
    rows_ref[...] = rows
    inner_ref[...] = (swish * upper).astype(BF)
    dgate_ref[...] = gate_grad
    dup_ref[...] = up_grad
    df_ref[...] = df
    da_ref[:, :D] = da
    da_ref[:, D:] = jnp.zeros((SPAN, 2 * LANES - D), BF)
    return middle_grad, nt(da, w_out).T.astype(BF)


def query_back(dq, cosine, sine):
    parts = [turn_back(head_rows(dq, j), cosine, sine) for j in range(HEADS)]
    return jnp.concatenate(parts, 0).T.astype(BF)


def entry_back(hidden, gain, w_qkv, cosine, sine, query_grad, dkv, middle_grad, rows_ref, dqkv_ref, gain_ref):
    turned = sum(part[...].astype(F32) for part in dkv).T
    parts = [turn_back(head_rows(turned, 2 * g), cosine, sine) for g in range(KV_HEADS)]
    parts += [head_rows(turned, 2 * g + 1) for g in range(KV_HEADS)]
    kv_grad = jnp.concatenate(parts, 0).T.astype(BF)
    grads = jnp.concatenate([query_grad.astype(F32), kv_grad.astype(F32)], 1).astype(BF)
    normed, inverse, rows = attn_rows(hidden, gain)
    rows_grad = nt(grads, w_qkv)
    rows_ref[...] = rows
    dqkv_ref[...] = grads
    gain_ref[...] = jnp.sum(rows_grad * normed, 0, keepdims=True)
    return middle_grad + norm_back(rows_grad * gain, normed, inverse)


VM = pl.BlockSpec(memory_space=pltpu.VMEM)
HBM = pl.BlockSpec(memory_space=pl.ANY)
HALF = D // 2
QUARTER = HALF // 2
A_WIDTH = QKV
B_PART = 1408
B_WIDTH = 4 * B_PART
DOWN_AT = 2 * FF
OUT_AT = 3 * FF


def shape(dims, kind=BF):
    return jax.ShapeDtypeStruct(dims, kind)


def here():
    place = lax.axis_index("ctx")
    return place // 8, lax.rem(place // 2, 4), lax.rem(place, 2)


def start_quarters(layer, sources, copies_of, far_copies_of):
    own, near, far, across, near_twin, far_twin, across_twin = sources
    section, half = lax.axis_index("section"), lax.axis_index("wsh")
    core = here()[2]
    home, away = [], []
    for m, place in enumerate((core, 1 - core)):
        home += copies_of(own, place * QUARTER, True, half, place, m)
        home += far_copies_of(far_twin if m else far, 1 - half, place, 2 + m)
        away += copies_of(near_twin if m else near, 0, False, half, place, m)
        away += copies_of(across_twin if m else across, 0, False, 1 - half, place, 2 + m)

    @pl.when(section == layer)
    def _():
        for copy in home:
            copy.start()

    @pl.when(section != layer)
    def _():
        for copy in away:
            copy.start()

    return away


def rows_at(start, size):
    if isinstance(start, int):
        return pl.ds(start, size)
    return pl.ds(pl.multiple_of(start, 16), size)


def fetch_a(layer, sources, matrix, gains, sems):
    def copies_of(source, first, whole, rows, place, k):
        gain_at = HALF if whole else QUARTER
        out = [
            pltpu.make_async_copy(
                source.at[rows_at(first, QUARTER)],
                matrix.at[rows_at(rows * HALF + place * QUARTER, QUARTER)],
                sems.at[k],
            )
        ]
        if k % 2 == 0:
            out.append(
                pltpu.make_async_copy(
                    source.at[rows_at(gain_at, 16)], gains.at[rows_at(rows * 16, 16)], sems.at[4 + k // 2]
                )
            )
        return out

    def far_copies_of(source, rows, place, k):
        return copies_of(source, 0, False, rows, place, k)

    return start_quarters(layer, sources, copies_of, far_copies_of)


def gain_rows(gains):
    values = gains[...].astype(F32)
    return [
        jnp.concatenate([values[0:1, at : at + HALF], values[16:17, at : at + HALF]], 1) for at in (0, 384)
    ]


def fetch_b(layer, sources, matrix, sems):
    y, x, core = here()

    def copies_of(source, first, whole, rows, place, k):
        return [
            pltpu.make_async_copy(
                source.at[rows_at(first, QUARTER)],
                matrix.at[rows_at(rows * HALF + place * QUARTER, QUARTER)],
                sems.at[k],
            )
        ]

    def far_copies_of(source, rows, place, k):
        at = jnp.where(place == 0, y, x)
        return [
            pltpu.make_async_copy(
                source.at[back],
                matrix.at[
                    rows_at(rows * HALF + place * QUARTER, QUARTER),
                    pl.ds(pl.multiple_of(lax.rem(at + 4 - back, 4) * B_PART, 128), B_PART),
                ],
                sems.at[k],
            )
            for back in range(4)
        ]

    return start_quarters(layer, sources, copies_of, far_copies_of)


def wait_all(copies):
    for copy in copies:
        copy.wait()


A_SCRATCH = [pltpu.VMEM((D, A_WIDTH), BF), pltpu.VMEM((32, A_WIDTH), BF), pltpu.SemaphoreType.DMA((6,))]
B_SCRATCH = [pltpu.VMEM((D, B_WIDTH), BF), pltpu.SemaphoreType.DMA((4,))]


def b_values(matrix):
    halves = [
        jnp.concatenate([matrix[low : low + HALF, at : at + FF // 2] for at in (DOWN_AT, DOWN_AT + FF // 2)], 0)
        for low in (0, HALF)
    ]
    return matrix[:, :FF], matrix[:, FF : 2 * FF], halves, matrix[:, OUT_AT : OUT_AT + D]


def call(kernel, ins, out_shape, scratch, flops, out_spec=VM):
    specs = [spec for spec, arrays in ins for _ in arrays]
    arrays = [array for _, arrays in ins for array in arrays]
    return pl.pallas_call(
        kernel,
        in_specs=specs,
        out_specs=[out_spec] * len(out_shape),
        out_shape=out_shape,
        scratch_shapes=scratch,
        compiler_params=pltpu.CompilerParams(vmem_limit_bytes=VMEM_LIMIT),
        cost_estimate=pl.CostEstimate(flops=flops, bytes_accessed=12_000_000, transcendentals=5_000_000),
    )(*arrays)


QUERY = shape((KV_HEADS, HEAD_DIM, ROWS))
OWN = shape((SPAN, KVW))
TOKENS = shape((SPAN, D))
TURNED = shape((D, SPAN))
TURNED32 = shape((D, SPAN), F32)
TOKENS32 = shape((SPAN, D), F32)
MIXED = shape((KV_HEADS, HEAD_DIM, ROWS))
LOGS = shape((8, ROWS), F32)
GAIN = shape((1, D), F32)
WIDE = shape((SPAN, FF))
FEED_BACK = [TOKENS, WIDE, WIDE, WIDE, TOKENS, shape((SPAN, 768)), GAIN]
PIECE = shape((BLOCK, KVW))


def read_turned(ref):
    return ref[...].astype(F32).T


def open_kernel(x_ref, cos_ref, sin_ref, *refs):
    a, (query_ref, kv_ref), (wqkv, gains, sems) = refs[:7], refs[7:9], refs[9:]
    copies = fetch_a(0, a, wqkv, gains, sems)
    cosine, sine = cos_ref[...], sin_ref[...]
    normed, _ = normalize(read_turned(x_ref))
    wait_all(copies)
    project((normed * gain_rows(gains)[0]).astype(BF), wqkv[...], cosine, sine, query_ref, kv_ref)


def first_kernel(*refs):
    kv_refs, refs = refs[:PIECES], refs[PIECES:]
    (x_ref, query_ref, bias_ref, tri_ref, cos_ref, sin_ref), refs = refs[:6], refs[6:]
    a, b, refs = refs[:7], refs[7:14], refs[14:]
    (act_ref, mixed_ref, logs_ref, middle_ref, query1_ref, kv1_ref), refs = refs[:6], refs[6:]
    a_scr, a0_scr, b_scr = refs[:3], refs[3:6], refs[6:]
    copies_b = fetch_b(0, b, *b_scr)
    copies_a0 = fetch_a(0, a, *a0_scr)
    copies_a = fetch_a(1, a, *a_scr)
    mixed, logs = attend(query_ref, kv_refs, bias_ref[...], tri_ref[...])
    for g in range(KV_HEADS):
        mixed_ref[g] = mixed[g]
        logs_ref[g : g + 1] = logs[g]
    wait_all(copies_b + copies_a0 + copies_a)
    w_gate, w_up, w_down, w_out = b_values(b_scr[0])
    flat = ungroup([m.astype(F32) for m in mixed]).T.astype(BF)
    middle = read_turned(x_ref) + nn(flat, w_out)
    middle_ref[...] = middle
    _, _, _, gate, upper = feed(middle, gain_rows(a0_scr[1])[1], w_gate, w_up)
    inner = (jax.nn.silu(gate) * upper).astype(BF)
    act = (middle + down(inner, w_down)).astype(BF)
    act_ref[...] = act.astype(F32).T.astype(BF)
    _, _, rows = attn_rows(act.astype(F32), gain_rows(a_scr[1])[0])
    project(rows, a_scr[0][...], cos_ref[...], sin_ref[...], query1_ref, kv1_ref)


def second_kernel(*refs):
    kv_refs, refs = refs[:PIECES], refs[PIECES:]
    (x_ref, cot_ref, query_ref, bias_ref, tri_ref, cos_ref, sin_ref), refs = refs[:7], refs[7:]
    a, b, refs = refs[:7], refs[7:14], refs[14:]
    (act_ref, flat_ref, dh2_ref, dq_ref), refs = refs[:4], refs[4:]
    back_refs, refs = refs[:7], refs[7:]
    dkv_refs, refs = refs[:PIECES], refs[PIECES:]
    a_scr, b_scr = refs[:3], refs[3:]
    copies_b = fetch_b(1, b, *b_scr)
    copies_a = fetch_a(1, a, *a_scr)
    bias, triangle = bias_ref[...], tri_ref[...]
    mixed, logs = attend(query_ref, kv_refs, bias, triangle)
    wait_all(copies_b + copies_a)
    w_gate, w_up, w_down, w_out = b_values(b_scr[0])
    flat = ungroup([m.astype(F32) for m in mixed]).T.astype(BF)
    flat_ref[...] = flat
    middle = read_turned(x_ref) + nn(flat, w_out)
    gain = gain_rows(a_scr[1])[1]
    parts = feed(middle, gain, w_gate, w_up)
    dh2, do = feed_back(read_turned(cot_ref), middle, gain, w_gate, w_up, w_down, w_out, parts, back_refs)
    act_ref[...] = (middle + down(back_refs[1][...], w_down)).T.astype(BF)
    dh2_ref[...] = dh2
    dq = attend_back(query_ref, kv_refs, bias, triangle, mixed, logs, do, dkv_refs)
    dq_ref[...] = query_back(dq, cos_ref[...], sin_ref[...])


def third_kernel(*refs):
    kv_refs, refs = refs[:PIECES], refs[PIECES:]
    own_dkv, refs = refs[:4], refs[4:]
    (act_ref, dh2_ref, dq_ref, mixed_ref, logs_ref, middle_ref, query_ref), refs = refs[:7], refs[7:]
    (bias_ref, tri_ref, cos_ref, sin_ref), refs = refs[:4], refs[4:]
    a, b, refs = refs[:7], refs[7:14], refs[14:]
    (grad1_ref, rows1_ref, dqkv1_ref, gain1_ref), refs = refs[:4], refs[4:]
    (flat_ref, dh2_out_ref, dq_out_ref), refs = refs[:3], refs[3:]
    back_refs, refs = refs[:7], refs[7:]
    dkv_refs, refs = refs[:PIECES], refs[PIECES:]
    a_scr, a0_scr, b_scr = refs[:3], refs[3:6], refs[6:]
    copies_a = fetch_a(1, a, *a_scr)
    copies_a0 = fetch_a(0, a, *a0_scr)
    copies_b = fetch_b(0, b, *b_scr)
    cosine, sine = cos_ref[...], sin_ref[...]
    wait_all(copies_a)
    grad = entry_back(
        read_turned(act_ref), gain_rows(a_scr[1])[0], a_scr[0][...], cosine, sine,
        dq_ref[...], own_dkv, dh2_ref[...], rows1_ref, dqkv1_ref, gain1_ref,
    )
    grad1_ref[...] = grad.T
    wait_all(copies_a0 + copies_b)
    w_gate, w_up, w_down, w_out = b_values(b_scr[0])
    mixed = [mixed_ref[g] for g in range(KV_HEADS)]
    logs = [logs_ref[g : g + 1] for g in range(KV_HEADS)]
    flat_ref[...] = ungroup([m.astype(F32) for m in mixed]).T.astype(BF)
    gain = gain_rows(a0_scr[1])[1]
    middle = middle_ref[...]
    parts = feed(middle, gain, w_gate, w_up)
    dh2, do = feed_back(
        grad.astype(BF).astype(F32), middle, gain, w_gate, w_up, w_down, w_out, parts, back_refs
    )
    dh2_out_ref[...] = dh2
    dq = attend_back(query_ref, kv_refs, bias_ref[...], tri_ref[...], mixed, logs, do, dkv_refs)
    dq_out_ref[...] = query_back(dq, cosine, sine)


def close_kernel(*refs):
    own_dkv, refs = refs[:4], refs[4:]
    (x_ref, dh2_ref, dq_ref, cos_ref, sin_ref), refs = refs[:5], refs[5:]
    a, refs = refs[:7], refs[7:]
    (grad_ref, rows_ref, dqkv_ref, gain_ref), a_scr = refs[:4], refs[4:]
    copies = fetch_a(0, a, *a_scr)
    wait_all(copies)
    grad = entry_back(
        read_turned(x_ref), gain_rows(a_scr[1])[0], a_scr[0][...], cos_ref[...], sin_ref[...],
        dq_ref[...], own_dkv, dh2_ref[...], rows_ref, dqkv_ref, gain_ref,
    )
    grad_ref[...] = grad.T


LANES = 384
CHUNKS = 32


def on_the_way(chunk):
    y, x, core = here()
    to_y, to_x, to_core = chunk // 8, chunk // 2 % 4, chunk % 2
    back_y, back_x = lax.rem(y + 4 - to_y, 4), lax.rem(x + 4 - to_x, 4)
    at = back_x * 4 + back_y if to_core == 0 else back_y * 4 + back_x
    return at, core == to_core


def put_chunk(mine_ref, theirs_ref, chunk, value):
    at, stays = on_the_way(chunk)

    @pl.when(stays)
    def _():
        mine_ref[at] = value

    @pl.when(jnp.logical_not(stays))
    def _():
        theirs_ref[at] = value


def send_chunk(held, mine_ref, theirs_ref, sems, chunk):
    at, stays = on_the_way(chunk)
    mine = pltpu.make_async_copy(held.at[chunk], mine_ref.at[at], sems.at[chunk])
    theirs = pltpu.make_async_copy(held.at[chunk], theirs_ref.at[at], sems.at[chunk])

    @pl.when(stays)
    def _():
        mine.start()

    @pl.when(jnp.logical_not(stays))
    def _():
        theirs.start()

    return mine


def feed_grads_kernel(
    flat_ref, da_ref, rows_ref, dgate_ref, dup_ref, inner_ref, df_ref, mine_ref, theirs_ref, held, sems
):
    rows = rows_ref[...].astype(F32).T.astype(BF)
    flat = flat_ref[...].astype(F32).T.astype(BF)
    df = df_ref[...].astype(F32).T.astype(BF)
    copies = []

    def sent(j):
        for r in range(2):
            copies.append(send_chunk(held, mine_ref, theirs_ref, sems, r * 16 + j))

    def put(value, j):
        for half in range(2):
            for r in range(2):
                at = half * HALF + r * QUARTER
                held[r * 16 + j, half] = value[at : at + QUARTER].astype(BF)
        sent(j)

    empty = jnp.zeros((QUARTER, LANES), BF)
    for j in (14, 15):
        for half in range(2):
            for r in range(2):
                held[r * 16 + j, half] = empty
        sent(j)
    for j in range(4):
        lanes = slice(j * LANES, (j + 1) * LANES)
        put(nn(rows, dgate_ref[:, lanes]), j)
        put(nn(rows, dup_ref[:, lanes]), 4 + j)
    for j in range(2):
        for half in range(2):
            at = half * (FF // 2) + j * LANES
            value = nn(df, inner_ref[:, at : at + LANES])
            for top in range(2):
                for r in range(2):
                    line = top * HALF + r * QUARTER
                    held[r * 16 + 8 + 2 * top + j, half] = value[line : line + QUARTER].astype(BF)
        sent(8 + j)
        sent(10 + j)
    put(nn(flat, da_ref[:, :LANES]), 12)
    put(nn(flat, da_ref[:, LANES:]), 13)
    wait_all(copies)


def entry_grads_kernel(*refs):
    mine_ref, theirs_ref = refs[8:]
    values = []
    for layer in range(2):
        rows_ref, dqkv_ref, gain_attn_ref, gain_mlp_ref = refs[4 * layer : 4 * layer + 4]
        rows = rows_ref[...].astype(F32).T.astype(BF)
        value = nn(rows, dqkv_ref[...])
        gains = jnp.concatenate(
            [gain_attn_ref[...], gain_mlp_ref[...], jnp.zeros((HEAD_DIM - 2, D), F32)], 0
        ).T
        values.append(jnp.concatenate([value, gains], 1).astype(BF))
    for r in range(2):
        for j in range(16):
            lanes = slice(j * HEAD_DIM, (j + 1) * HEAD_DIM)
            parts = [
                value[half * HALF + r * QUARTER : half * HALF + (r + 1) * QUARTER, lanes]
                for value in values
                for half in range(2)
            ]
            put_chunk(mine_ref, theirs_ref, r * 16 + j, jnp.concatenate(parts, 1))


def unpack_kernel(*refs):
    came, refs = refs[:8], refs[8:]
    (norms_ref, query_ref, key_ref, value_ref, out_ref, gate_ref, up_ref, down_ref), (held,) = refs[:8], refs[8:]
    y, x, core = here()
    for piece in range(8):
        which = core if piece < 4 else 1 - core
        k2 = piece % 4
        for k1 in range(4):
            back_y = jnp.where(which == 0, k1, k2)
            back_x = jnp.where(which == 0, k2, k1)
            chunk = lax.rem(y + 4 - back_y, 4) * 8 + lax.rem(x + 4 - back_x, 4) * 2 + which
            held[chunk] = came[piece][k1]
    for r in range(2):
        rows = slice(r * QUARTER, (r + 1) * QUARTER)

        def block(j):
            return held[r * 16 + j, :, :LANES].astype(F32)

        def head(j):
            return held[r * 16 + j, :, LANES:].astype(F32)

        for j in range(4):
            lanes = slice(j * LANES, (j + 1) * LANES)
            gate_ref[rows, lanes] = block(j)
            up_ref[rows, lanes] = block(4 + j)
        for j in range(2):
            lanes = slice(j * LANES, (j + 1) * LANES)
            for top in range(2):
                down_ref[top * HALF + r * QUARTER : top * HALF + (r + 1) * QUARTER, lanes] = block(8 + 2 * top + j)
        out_ref[rows] = jnp.concatenate([block(12), block(13)[:, : D - LANES]], 1)
        query_ref[rows] = jnp.concatenate([head(j) for j in range(HEADS)], 1)
        key_ref[rows] = jnp.concatenate([head(HEADS + j) for j in range(KV_HEADS)], 1)
        value_ref[rows] = jnp.concatenate([head(HEADS + KV_HEADS + j) for j in range(KV_HEADS)], 1)
    turned = jnp.concatenate([held[r * 16 + 15, :, LANES:].astype(F32).T for r in range(2)], 1)
    norms_ref[...] = turned[:8]


def routes(axes_size):
    def turn_of(i, along_y, k):
        core, x, y = i % 2, i // 2 % 4, i // 8
        if along_y:
            y = (y + k) % 4
        else:
            x = (x + k) % 4
        return y * 8 + x * 2 + core

    def first(k):
        return [(i, turn_of(i, i % 2 == 0, k)) for i in range(axes_size)]

    def second(k):
        return [(i, turn_of(i, i % 2 == 1, k)) for i in range(axes_size)]

    return first, second, [(i, i ^ 1) for i in range(axes_size)]


def per_device(
    inputs, cotangent, positions, norm_attn, w_query, w_key, w_value, w_out, norm_mlp, w_gate, w_up, w_down
):
    section = lax.axis_index("section")
    place = lax.axis_index("ctx")
    core = place % 2
    first, second, swap = routes(lax.axis_size("ctx"))

    def hop(block, route):
        return lax.ppermute(block, "ctx", route)

    def along_z(block, flip):
        return lax.ppermute(block, ("section", "wsh"), [(i, i ^ flip) for i in range(4)])

    spots = lax.dynamic_index_in_dim(positions, section, 0, keepdims=False)[0]
    gains = jnp.concatenate(
        [norm_attn, jnp.zeros((1, 96), BF), norm_mlp, jnp.zeros((1, A_WIDTH - 384 - HALF), BF)], 1
    )
    gains = jnp.concatenate([gains, jnp.zeros((15, A_WIDTH), BF)], 0)
    own_a = jnp.concatenate([w_query[0], w_key[0], w_value[0]], 1)
    half_a = jnp.concatenate([lax.dynamic_slice_in_dim(own_a, core * QUARTER, QUARTER, 0), gains], 0)
    own_a = jnp.concatenate([own_a, gains], 0)
    turned = w_down[0].T
    own_b = jnp.concatenate(
        [w_gate[0], w_up[0], turned[:HALF], turned[HALF:], w_out[0], jnp.zeros((HALF, B_WIDTH - OUT_AT - D), BF)], 1
    )
    half_b = lax.dynamic_slice_in_dim(own_b, core * QUARTER, QUARTER, 0)

    came = [along_z(half_a, flip) for flip in (2, 1, 3)]
    a = [own_a] + came + [hop(block, swap) for block in came]
    starts = lax.all_gather(spots[::RUN], "ctx", axis=0, tiled=True)

    x = lax.dynamic_index_in_dim(inputs, section, 0, keepdims=False)[0].T
    cot = lax.dynamic_index_in_dim(cotangent, section, 0, keepdims=False)[0].T
    freq = BASE ** (-(jnp.arange(HEAD_DIM // 2, dtype=F32) * 2.0 / HEAD_DIM))
    angle = freq[:, None] * spots.astype(F32)[None, :]
    cosine, sine = jnp.cos(angle), jnp.sin(angle)
    triangle = jnp.where(spots[:, None] <= spots[None, :], 0.0, NEG).astype(F32)

    k1, k2 = jnp.arange(4)[None, :], jnp.arange(4)[:, None]
    y, x_at = place // 8, place // 2 % 4

    def origin(which):
        back_y = jnp.where(which == 0, k1, k2)
        back_x = jnp.where(which == 0, k2, k1)
        return ((y - back_y) % 4 * 8 + (x_at - back_x) % 4 * 2 + which).reshape(16)

    order = jnp.concatenate([origin(core), origin(1 - core)])
    picked = order[:, None] == jnp.arange(CHUNKS)[None, :]
    starts = jnp.sum(jnp.where(picked[:, :, None], starts.reshape(1, CHUNKS, 2), 0), 1).reshape(RUNS)
    open_run = (starts[:, None] < (spots - spots % RUN)[None, :]) & (jnp.arange(RUNS)[:, None] > 1)
    bias = jnp.tile(jnp.where(open_run, 0.0, NEG), (1, GROUP)).astype(BF)

    def gathered(own):
        four = jnp.concatenate([own] + [hop(own, first(k)) for k in (1, 2, 3)], 0)
        mine = [four] + [hop(four, second(k)) for k in (1, 2, 3)]
        return mine + [hop(piece, swap) for piece in mine]

    def summed(pieces):
        def add(*parts):
            return sum(part.astype(F32) for part in parts).astype(BF)

        mine = [add(pieces[k], hop(pieces[4 + k], swap)) for k in range(4)]
        four = add(mine[0], *[hop(mine[k], second(-k)) for k in (1, 2, 3)])
        parts = [four[k * SPAN : (k + 1) * SPAN] for k in range(4)]
        return [parts[0]] + [hop(parts[k], first(-k)) for k in (1, 2, 3)]

    def ring(block):
        return jnp.stack([block] + [hop(block, first(k)) for k in (1, 2, 3)])

    half_b, *_ = lax.optimization_barrier((half_b, *a[1:4]))
    near, across = along_z(half_b, 2), along_z(half_b, 3)
    ring_place = jnp.where(core == 0, y, x_at)
    part = lax.dynamic_slice_in_dim(half_b, ring_place * B_PART, B_PART, 1)
    far = ring(along_z(part, 1))
    b = [own_b, near, far, across] + [hop(block, swap) for block in (near, far, across)]
    x, bias = lax.optimization_barrier((x, bias))
    query0, own0 = call(
        open_kernel, [(VM, [x, cosine, sine]), (HBM, a)], [QUERY, OWN], A_SCRATCH, 10**8
    )
    all0 = gathered(own0)
    act0, mixed0, logs0, middle0, query1, own1 = call(
        first_kernel,
        [(VM, all0 + [x, query0, bias, triangle, cosine, sine]), (HBM, a + b)],
        [TURNED, MIXED, LOGS, TOKENS32, QUERY, OWN],
        A_SCRATCH + A_SCRATCH + B_SCRATCH,
        2 * 10**9,
    )
    all1 = gathered(own1)
    act1, flat, dh2, dq, rows, inner, dgate, dup, df, da, gain_mlp1, *dkv = call(
        second_kernel,
        [(VM, all1 + [act0, cot, query1, bias, triangle, cosine, sine]), (HBM, a + b)],
        [TURNED, TOKENS, TOKENS32, TOKENS] + FEED_BACK + [PIECE] * PIECES,
        A_SCRATCH + B_SCRATCH,
        7 * 10**9,
    )
    def add(*parts):
        return sum(part.astype(F32) for part in parts).astype(BF)

    def to_cores(mine, theirs):
        came = hop(theirs, swap)
        return [add(mine[4 * k : 4 * k + 4], came[4 * k : 4 * k + 4]) for k in range(4)]

    def to_rings(sets):
        came = [hop(sets[k], second(-k)) for k in (1, 2, 3)]
        return [add(sets[0][k], *[block[k] for block in came]) for k in range(4)]

    def to_place(blocks):
        return add(blocks[0], *[hop(blocks[k], first(-k)) for k in (1, 2, 3)])

    FEED_SCRATCH = [pltpu.VMEM((CHUNKS, 2, QUARTER, LANES), BF), pltpu.SemaphoreType.DMA((CHUNKS,))]
    FEEDS = [shape((16, 2, QUARTER, LANES))] * 2
    ENTRIES = [shape((16, QUARTER, 4 * HEAD_DIM))] * 2
    own_dkv = summed(dkv)
    feed1 = call(feed_grads_kernel, [(VM, [flat, da, rows, dgate, dup, inner, df])], FEEDS, FEED_SCRATCH, 10**9, HBM)
    feed1 = to_cores(*feed1)
    dq, *feed1 = lax.optimization_barrier((dq, *feed1))
    feed1 = to_rings(feed1)
    (
        grad1, rows_in1, dqkv1, gain_attn1,
        flat, dh2, dq, rows, inner, dgate, dup, df, da, gain_mlp0, *dkv,
    ) = call(
        third_kernel,
        [
            (VM, all0 + own_dkv + [act0, dh2, dq, mixed0, logs0, middle0, query0]),
            (VM, [bias, triangle, cosine, sine]),
            (HBM, a + b),
        ],
        [TURNED32, TOKENS, shape((SPAN, QKV)), GAIN]
        + [TOKENS, TOKENS32, TOKENS]
        + FEED_BACK
        + [PIECE] * PIECES,
        A_SCRATCH + A_SCRATCH + B_SCRATCH,
        6 * 10**9,
    )
    own_dkv = summed(dkv)
    feed1 = to_place(feed1)
    feed0 = call(feed_grads_kernel, [(VM, [flat, da, rows, dgate, dup, inner, df])], FEEDS, FEED_SCRATCH, 10**9, HBM)
    feed0 = to_place(to_rings(to_cores(*feed0)))
    grad0, rows_in0, dqkv0, gain_attn0 = call(
        close_kernel,
        [(VM, own_dkv + [x, dh2, dq, cosine, sine]), (HBM, a)],
        [TURNED32, TOKENS, shape((SPAN, QKV)), GAIN],
        A_SCRATCH,
        10**8,
    )
    entries = call(
        entry_grads_kernel,
        [(VM, [rows_in0, dqkv0, gain_attn0, gain_mlp0, rows_in1, dqkv1, gain_attn1, gain_mlp1])],
        ENTRIES,
        [],
        10**8,
    )
    entries = to_place(to_rings(to_cores(*entries)))

    entries = entries.reshape(QUARTER, 2, 2, HEAD_DIM).transpose(1, 2, 0, 3)
    every = jnp.concatenate([jnp.stack([feed0, feed1]), entries], -1).reshape(4, QUARTER, LANES + HEAD_DIM)
    spot = section * 2 + lax.axis_index("wsh")

    def chunk(flip):
        return lax.dynamic_index_in_dim(every, spot ^ flip, 0, keepdims=False)

    total = add(chunk(0), *[along_z(chunk(flip), flip) for flip in (1, 2, 3)])
    four = jnp.stack([total] + [hop(total, first(k)) for k in (1, 2, 3)])
    mine = [four] + [hop(four, second(k)) for k in (1, 2, 3)]
    came = mine + [hop(piece, swap) for piece in mine]
    norms, g_query, g_key, g_value, g_out, g_gate, g_up, g_down = call(
        unpack_kernel,
        [(VM, came)],
        [
            shape((8, HALF), F32), shape((HALF, D), F32), shape((HALF, KVW // 2), F32), shape((HALF, KVW // 2), F32),
            shape((HALF, D), F32), shape((HALF, FF), F32), shape((HALF, FF), F32), shape((D, FF // 2), F32),
        ],
        [pltpu.VMEM((CHUNKS, QUARTER, LANES + HEAD_DIM), BF)],
        10**8,
    )

    def exchanged(own, other):
        kept = jnp.where(section == 0, own, other)
        sent = jnp.where(section == 0, other, own)
        came = lax.ppermute(sent, "section", [(0, 1), (1, 0)])
        return jnp.where(section == 0, jnp.stack([kept, came]), jnp.stack([came, kept]))

    acts = exchanged(act0, act1)
    grads = exchanged(grad0, grad1)
    return (
        acts.swapaxes(1, 2)[None, :, None],
        grads.swapaxes(1, 2)[None, :, None],
        norms[0:1],
        g_query[None],
        g_key[None],
        g_value[None],
        g_out[None],
        norms[1:2],
        g_gate[None],
        g_up[None],
        g_down.T[None],
    )


def solution(mesh):
    placed = (
        P(None, "wsh", "ctx", None),
        P(None, "wsh", "ctx", None),
        P(None, "wsh", "ctx"),
        P("section", "wsh"),
        P("section", "wsh", None),
        P("section", "wsh", None),
        P("section", "wsh", None),
        P("section", "wsh", None),
        P("section", "wsh"),
        P("section", "wsh", None),
        P("section", "wsh", None),
        P("section", "wsh", None),
    )
    return jax.shard_map(
        per_device,
        mesh=mesh,
        in_specs=placed,
        out_specs=(
            P("section", None, "wsh", "ctx", None),
            P("section", None, "wsh", "ctx", None),
            P("section", "wsh"),
            P("section", "wsh", None),
            P("section", "wsh", None),
            P("section", "wsh", None),
            P("section", "wsh", None),
            P("section", "wsh"),
            P("section", "wsh", None),
            P("section", "wsh", None),
            P("section", "wsh", None),
        ),
        check_vma=False,
    )
```

```python
import jax
import jax.numpy as jnp
from jax import lax
from jax.experimental import pallas as pl
from jax.experimental.pallas import tpu as pltpu
from jax.sharding import PartitionSpec as P

HEADS = 9
KV_HEADS = 3
GROUP = HEADS // KV_HEADS
HEAD_DIM = 64
D = HEADS * HEAD_DIM
FF = 1536
QKV = D + 2 * KV_HEADS * HEAD_DIM
KVW = 2 * KV_HEADS * HEAD_DIM
SPAN = 128
RUN = 64
LENGTH = 4096
RUNS = LENGTH // RUN
ROWS = GROUP * SPAN
BLOCK = 512
PIECES = LENGTH // BLOCK
PER_PIECE = BLOCK // SPAN
MARKED = SPAN + 16

EPS = 1e-05
NEG = -1e30
BASE = 100000.0
SCALE = HEAD_DIM ** (-0.5)

BF = jnp.bfloat16
F32 = jnp.float32
VMEM_LIMIT = 56 * 1024 * 1024


def nn(left, right):
    return lax.dot_general(left, right, (((1,), (0,)), ((), ())), preferred_element_type=F32)


def nt(left, right):
    return lax.dot_general(left, right, (((1,), (1,)), ((), ())), preferred_element_type=F32)


def normalize(hidden):
    inverse = lax.rsqrt(jnp.mean(hidden * hidden, -1, keepdims=True) + EPS)
    return hidden * inverse, inverse


def norm_back(grad, normed, inverse):
    return inverse * (grad - normed * jnp.mean(grad * normed, -1, keepdims=True))


def turn(head, cosine, sine):
    half = HEAD_DIM // 2
    first, second = head[:half], head[half:]
    return jnp.concatenate([first * cosine - second * sine, second * cosine + first * sine], 0)


def turn_back(head, cosine, sine):
    half = HEAD_DIM // 2
    first, second = head[:half], head[half:]
    return jnp.concatenate([first * cosine + second * sine, second * cosine - first * sine], 0)


def head_rows(array, head):
    return array[head * HEAD_DIM : (head + 1) * HEAD_DIM]


def group_of(array, group):
    return jnp.concatenate([head_rows(array, group * GROUP + r) for r in range(GROUP)], 1)


def ungroup(parts):
    return jnp.concatenate(
        [parts[g][:, r * SPAN : (r + 1) * SPAN] for g in range(KV_HEADS) for r in range(GROUP)], 0
    )


def attn_rows(hidden, gain):
    normed, inverse = normalize(hidden)
    return normed, inverse, (normed * gain).astype(BF)


def project(rows, w_qkv, cosine, sine, query_ref, kv_ref):
    flat = nn(rows, w_qkv).T
    heads = [turn(head_rows(flat, j), cosine, sine) * SCALE for j in range(HEADS)]
    for g in range(KV_HEADS):
        query_ref[g] = jnp.concatenate(heads[g * GROUP : (g + 1) * GROUP], 1).astype(BF)
    parts = []
    for g in range(KV_HEADS):
        parts.append(turn(head_rows(flat, HEADS + g), cosine, sine))
        parts.append(head_rows(flat, HEADS + KV_HEADS + g))
    kv_ref[...] = jnp.concatenate(parts, 0).T.astype(BF)


def one_hot(first_run, rows):
    lane = lax.broadcasted_iota(jnp.int32, (rows, SPAN), 1)
    run = lax.broadcasted_iota(jnp.int32, (rows, SPAN), 0) // RUN + first_run
    marked = (lane == run) | ((lane >= RUNS) & (lane < RUNS + 3))
    return jnp.where(marked, 1.0, 0.0).astype(BF)


def columns(g):
    return slice(g * SPAN, (g + 1) * SPAN)


def key_rows(piece, skip, g):
    if piece.shape[0] == BLOCK:
        return piece[skip:, columns(g)]
    first = skip // SPAN
    return jnp.concatenate(
        [piece[k * MARKED : k * MARKED + SPAN, columns(g)] for k in range(first, PER_PIECE)], 0
    )


def attend(query_ref, kv_refs, bias, triangle):
    zeros = jnp.zeros((HEAD_DIM, ROWS), BF)
    fixed = [jnp.concatenate([query_ref[g], zeros, bias, zeros], 0) for g in range(KV_HEADS)]
    triangle = jnp.concatenate([triangle] * GROUP, 1)
    start = []
    for g in range(KV_HEADS):
        own = kv_refs[0][:SPAN, columns(g)]
        scores = nn(own, fixed[g][:SPAN]) + triangle
        top = jnp.max(scores, 0, keepdims=True)
        probs = jnp.exp(scores - top)
        start += [top, jnp.sum(probs, 0, keepdims=True), nn(own.T[HEAD_DIM:], probs.astype(BF))]

    def step(b, carry):
        skip = SPAN if b == 0 else 0
        marks = one_hot((b * BLOCK + skip) // RUN, BLOCK - skip)
        out = []
        for g in range(KV_HEADS):
            top, total, accum = carry[3 * g : 3 * g + 3]
            block = key_rows(kv_refs[b], skip, g)
            scores = nn(jnp.concatenate([block, marks], 1), fixed[g])
            higher = jnp.maximum(top, jnp.max(scores, 0, keepdims=True))
            probs = jnp.exp(scores - higher)
            fade = jnp.exp(top - higher)
            total = total * fade + jnp.sum(probs, 0, keepdims=True)
            accum = accum * fade + nn(block.T[HEAD_DIM:], probs.astype(BF))
            out += [higher, total, accum]
        return tuple(out)

    done = tuple(start)
    for b in range(PIECES):
        done = step(b, done)
    mixed = [(done[3 * g + 2] / done[3 * g + 1]).astype(BF) for g in range(KV_HEADS)]
    logs = [done[3 * g] + jnp.log(done[3 * g + 1]) for g in range(KV_HEADS)]
    return mixed, logs


def attend_back(query_ref, kv_refs, bias, triangle, mixed, logs, mixed_grad, dkv_refs):
    zeros = jnp.zeros((HEAD_DIM, ROWS), BF)
    row = lax.broadcasted_iota(jnp.int32, (HEAD_DIM, 2 * ROWS), 0)
    triangle = jnp.concatenate([triangle] * GROUP, 1)
    fixed, turned = [], []
    for g in range(KV_HEADS):
        grads = group_of(mixed_grad, g)
        delta = jnp.sum(grads.astype(F32) * mixed[g].astype(F32), 0, keepdims=True)
        less = -jnp.concatenate([logs[g], delta], 1)
        high = less.astype(BF).astype(F32)
        middle = (less - high).astype(BF).astype(F32)
        lowest = less - high - middle
        stats = jnp.where(row == 0, high, jnp.where(row == 1, middle, jnp.where(row == 2, lowest, 0.0)))
        both = jnp.concatenate(
            [jnp.concatenate([query_ref[g], zeros], 1), jnp.concatenate([zeros, grads], 1)], 0
        )
        fixed.append(
            jnp.concatenate([both, jnp.concatenate([bias, zeros], 1), stats.astype(BF)], 0)
        )
        turned.append(both.T)

    def terms(block, marks, g, extra):
        both = nn(jnp.concatenate([block, marks], 1), fixed[g])
        scores = both[:, :ROWS]
        if extra is not None:
            scores = scores + extra
        probs = jnp.exp(scores)
        score_grad = (probs * both[:, ROWS:]).astype(BF)
        kv_terms = nn(jnp.concatenate([score_grad, probs.astype(BF)], 1), turned[g])
        return kv_terms.astype(BF), nn(block.T[:HEAD_DIM], score_grad)

    sums = [jnp.zeros((HEAD_DIM, ROWS), F32)] * KV_HEADS
    for b in range(PIECES):
        skip = SPAN if b == 0 else 0
        marks = one_hot((b * BLOCK + skip) // RUN, BLOCK - skip)
        for g in range(KV_HEADS):
            kv_terms, query_terms = terms(key_rows(kv_refs[b], skip, g), marks, g, None)
            dkv_refs[b][skip:, columns(g)] = kv_terms
            sums[g] = sums[g] + query_terms
    marks = one_hot(2 * RUNS, SPAN)
    for g in range(KV_HEADS):
        kv_terms, query_terms = terms(kv_refs[0][:SPAN, columns(g)], marks, g, triangle)
        dkv_refs[0][:SPAN, columns(g)] = kv_terms
        sums[g] = sums[g] + query_terms
    return ungroup(sums) * SCALE


def feed(middle, gain, w_gate, w_up):
    normed, inverse = normalize(middle)
    rows = (normed * gain).astype(BF)
    return normed, inverse, rows, nn(rows, w_gate), nn(rows, w_up)


def down(inner, w_down):
    half = FF // 2
    return nt(inner[:, :half], w_down[0]) + nt(inner[:, half:], w_down[1])


def feed_back(outgrad, middle, gain, w_gate, w_up, w_down, w_out, parts, refs):
    normed, inverse, rows, gate, upper = parts
    rows_ref, inner_ref, dgate_ref, dup_ref, df_ref, da_ref, gain_ref = refs
    sigma = jax.nn.sigmoid(gate)
    swish = gate * sigma
    df = outgrad.astype(BF)
    inner_grad = jnp.concatenate([nn(df, w_down[i]) for i in range(2)], 1)
    gate_grad = (inner_grad * upper * sigma * (1.0 + gate * (1.0 - sigma))).astype(BF)
    up_grad = (inner_grad * swish).astype(BF)
    rows_grad = nt(gate_grad, w_gate) + nt(up_grad, w_up)
    gain_ref[...] = jnp.sum(rows_grad * normed, 0, keepdims=True)
    middle_grad = outgrad + norm_back(rows_grad * gain, normed, inverse)
    da = middle_grad.astype(BF)
    rows_ref[...] = rows
    inner_ref[...] = (swish * upper).astype(BF)
    dgate_ref[...] = gate_grad
    dup_ref[...] = up_grad
    df_ref[...] = df
    da_ref[:, :D] = da
    da_ref[:, D:] = jnp.zeros((SPAN, 2 * LANES - D), BF)
    return middle_grad, nt(da, w_out).T.astype(BF)


def query_back(dq, cosine, sine):
    parts = [turn_back(head_rows(dq, j), cosine, sine) for j in range(HEADS)]
    return jnp.concatenate(parts, 0).T.astype(BF)


def entry_back(hidden, gain, w_qkv, cosine, sine, query_grad, dkv, middle_grad, rows_ref, dqkv_ref, gain_ref):
    turned = sum(part[...].astype(F32) for part in dkv).T
    parts = [turn_back(head_rows(turned, 2 * g), cosine, sine) for g in range(KV_HEADS)]
    parts += [head_rows(turned, 2 * g + 1) for g in range(KV_HEADS)]
    kv_grad = jnp.concatenate(parts, 0).T.astype(BF)
    grads = jnp.concatenate([query_grad.astype(F32), kv_grad.astype(F32)], 1).astype(BF)
    normed, inverse, rows = attn_rows(hidden, gain)
    rows_grad = nt(grads, w_qkv)
    rows_ref[...] = rows
    dqkv_ref[...] = grads
    gain_ref[...] = jnp.sum(rows_grad * normed, 0, keepdims=True)
    return middle_grad + norm_back(rows_grad * gain, normed, inverse)


VM = pl.BlockSpec(memory_space=pltpu.VMEM)
HBM = pl.BlockSpec(memory_space=pl.ANY)
HALF = D // 2
QUARTER = HALF // 2
A_WIDTH = QKV
B_PART = 1408
B_WIDTH = 4 * B_PART
DOWN_AT = 2 * FF
OUT_AT = 3 * FF


def shape(dims, kind=BF):
    return jax.ShapeDtypeStruct(dims, kind)


def here():
    place = lax.axis_index("ctx")
    return place // 8, lax.rem(place // 2, 4), lax.rem(place, 2)


def start_quarters(layer, sources, copies_of, far_copies_of):
    own, near, far, across, near_twin, far_twin, across_twin = sources
    section, half = lax.axis_index("section"), lax.axis_index("wsh")
    core = here()[2]
    home, away = [], []
    for m, place in enumerate((core, 1 - core)):
        home += copies_of(own, place * QUARTER, True, half, place, m)
        home += far_copies_of(far_twin if m else far, 1 - half, place, 2 + m)
        away += copies_of(near_twin if m else near, 0, False, half, place, m)
        away += copies_of(across_twin if m else across, 0, False, 1 - half, place, 2 + m)

    @pl.when(section == layer)
    def _():
        for copy in home:
            copy.start()

    @pl.when(section != layer)
    def _():
        for copy in away:
            copy.start()

    return away


def rows_at(start, size):
    if isinstance(start, int):
        return pl.ds(start, size)
    return pl.ds(pl.multiple_of(start, 16), size)


def fetch_a(layer, sources, matrix, gains, sems):
    def copies_of(source, first, whole, rows, place, k):
        gain_at = HALF if whole else QUARTER
        out = [
            pltpu.make_async_copy(
                source.at[rows_at(first, QUARTER)],
                matrix.at[rows_at(rows * HALF + place * QUARTER, QUARTER)],
                sems.at[k],
            )
        ]
        if k % 2 == 0:
            out.append(
                pltpu.make_async_copy(
                    source.at[rows_at(gain_at, 16)], gains.at[rows_at(rows * 16, 16)], sems.at[4 + k // 2]
                )
            )
        return out

    def far_copies_of(source, rows, place, k):
        return copies_of(source, 0, False, rows, place, k)

    return start_quarters(layer, sources, copies_of, far_copies_of)


def gain_rows(gains):
    values = gains[...].astype(F32)
    return [
        jnp.concatenate([values[0:1, at : at + HALF], values[16:17, at : at + HALF]], 1) for at in (0, 384)
    ]


def fetch_b(layer, sources, matrix, sems):
    y, x, core = here()

    def copies_of(source, first, whole, rows, place, k):
        return [
            pltpu.make_async_copy(
                source.at[rows_at(first, QUARTER)],
                matrix.at[rows_at(rows * HALF + place * QUARTER, QUARTER)],
                sems.at[k],
            )
        ]

    def far_copies_of(source, rows, place, k):
        at = jnp.where(place == 0, y, x)
        return [
            pltpu.make_async_copy(
                source.at[back],
                matrix.at[
                    rows_at(rows * HALF + place * QUARTER, QUARTER),
                    pl.ds(pl.multiple_of(lax.rem(at + 4 - back, 4) * B_PART, 128), B_PART),
                ],
                sems.at[k],
            )
            for back in range(4)
        ]

    return start_quarters(layer, sources, copies_of, far_copies_of)


def wait_all(copies):
    for copy in copies:
        copy.wait()


A_SCRATCH = [pltpu.VMEM((D, A_WIDTH), BF), pltpu.VMEM((32, A_WIDTH), BF), pltpu.SemaphoreType.DMA((6,))]
B_SCRATCH = [pltpu.VMEM((D, B_WIDTH), BF), pltpu.SemaphoreType.DMA((4,))]


def b_values(matrix):
    halves = [
        jnp.concatenate([matrix[low : low + HALF, at : at + FF // 2] for at in (DOWN_AT, DOWN_AT + FF // 2)], 0)
        for low in (0, HALF)
    ]
    return matrix[:, :FF], matrix[:, FF : 2 * FF], halves, matrix[:, OUT_AT : OUT_AT + D]


def call(kernel, ins, out_shape, scratch, flops, in_hbm=0):
    specs = [spec for spec, arrays in ins for _ in arrays]
    arrays = [array for _, arrays in ins for array in arrays]
    return pl.pallas_call(
        kernel,
        in_specs=specs,
        out_specs=[VM] * (len(out_shape) - in_hbm) + [HBM] * in_hbm,
        out_shape=out_shape,
        scratch_shapes=scratch,
        compiler_params=pltpu.CompilerParams(vmem_limit_bytes=VMEM_LIMIT),
        cost_estimate=pl.CostEstimate(flops=flops // 1000, bytes_accessed=10_000, transcendentals=0),
    )(*arrays)


QUERY = shape((KV_HEADS, HEAD_DIM, ROWS))
OWN = shape((SPAN, KVW))
TOKENS = shape((SPAN, D))
TURNED = shape((D, SPAN))
TURNED32 = shape((D, SPAN), F32)
TOKENS32 = shape((SPAN, D), F32)
MIXED = shape((KV_HEADS, HEAD_DIM, ROWS))
LOGS = shape((8, ROWS), F32)
GAIN = shape((1, D), F32)
WIDE = shape((SPAN, FF))
GRAD_SCRATCH = [
    pltpu.VMEM((SPAN, D), BF),
    pltpu.VMEM((SPAN, FF), BF),
    pltpu.VMEM((SPAN, FF), BF),
    pltpu.VMEM((SPAN, FF), BF),
    pltpu.VMEM((SPAN, D), BF),
    pltpu.VMEM((SPAN, 768), BF),
    pltpu.VMEM((32, 2, QUARTER, 384), BF),
    pltpu.SemaphoreType.DMA((32,)),
]
FEEDS = [shape((16, 2, QUARTER, 384))] * 2
PIECE = shape((BLOCK, KVW))


def read_turned(ref):
    return ref[...].astype(F32).T


def open_kernel(x_ref, cos_ref, sin_ref, runs_ref, *refs):
    a, (query_ref, kv_ref), (wqkv, gains, sems) = refs[:7], refs[7:9], refs[9:]
    copies = fetch_a(0, a, wqkv, gains, sems)
    cosine, sine = cos_ref[...], sin_ref[...]
    normed, _ = normalize(read_turned(x_ref))
    kv_ref[SPAN:] = runs_ref[...]
    wait_all(copies)
    rows = (normed * gain_rows(gains)[0]).astype(BF)
    project(rows, wqkv[...], cosine, sine, query_ref, kv_ref.at[:SPAN])


def mix_kernel(*refs):
    kv_refs, refs = refs[:PIECES], refs[PIECES:]
    query_ref, runs_ref, tri_ref, mixed_ref, logs_ref, bias_ref = refs
    keys = jnp.concatenate(
        [
            piece[k * MARKED + SPAN : (k + 1) * MARKED].astype(F32)[:2]
            for piece in kv_refs
            for k in range(PER_PIECE)
        ],
        0,
    )
    order = lax.broadcasted_iota(jnp.int32, (RUNS, ROWS), 0)
    bias = jnp.where((keys < runs_ref[...]) & (order > 1), 0.0, NEG).astype(BF)
    bias_ref[...] = bias
    mixed, logs = attend(query_ref, kv_refs, bias, tri_ref[...])
    for g in range(KV_HEADS):
        mixed_ref[g] = mixed[g]
        logs_ref[g : g + 1] = logs[g]


def first_kernel(*refs):
    (x_ref, mixed_ref, cos_ref, sin_ref), refs = refs[:4], refs[4:]
    a, b, refs = refs[:7], refs[7:14], refs[14:]
    (act_ref, middle_ref, query1_ref, kv1_ref), refs = refs[:4], refs[4:]
    a_scr, a0_scr, b_scr = refs[:3], refs[3:6], refs[6:]
    copies_b = fetch_b(0, b, *b_scr)
    copies_a0 = fetch_a(0, a, *a0_scr)
    copies_a = fetch_a(1, a, *a_scr)
    hidden = read_turned(x_ref)
    flat = ungroup([mixed_ref[g].astype(F32) for g in range(KV_HEADS)]).T.astype(BF)
    wait_all(copies_b + copies_a0 + copies_a)
    w_gate, w_up, w_down, w_out = b_values(b_scr[0])
    middle = hidden + nn(flat, w_out)
    middle_ref[...] = middle
    _, _, _, gate, upper = feed(middle, gain_rows(a0_scr[1])[1], w_gate, w_up)
    inner = (jax.nn.silu(gate) * upper).astype(BF)
    act = (middle + down(inner, w_down)).astype(BF)
    act_ref[...] = act.astype(F32).T.astype(BF)
    _, _, rows = attn_rows(act.astype(F32), gain_rows(a_scr[1])[0])
    project(rows, a_scr[0][...], cos_ref[...], sin_ref[...], query1_ref, kv1_ref)


LANES = 384
CHUNKS = 32


def on_the_way(chunk):
    y, x, core = here()
    to_y, to_x, to_core = chunk // 8, chunk // 2 % 4, chunk % 2
    back_y, back_x = lax.rem(y + 4 - to_y, 4), lax.rem(x + 4 - to_x, 4)
    at = back_x * 4 + back_y if to_core == 0 else back_y * 4 + back_x
    return at, core == to_core


def put_chunk(mine_ref, theirs_ref, chunk, value):
    at, stays = on_the_way(chunk)

    @pl.when(stays)
    def _():
        mine_ref[at] = value

    @pl.when(jnp.logical_not(stays))
    def _():
        theirs_ref[at] = value


def send_chunk(held, mine_ref, theirs_ref, sems, chunk):
    at, stays = on_the_way(chunk)
    mine = pltpu.make_async_copy(held.at[chunk], mine_ref.at[at], sems.at[chunk])
    theirs = pltpu.make_async_copy(held.at[chunk], theirs_ref.at[at], sems.at[chunk])

    @pl.when(stays)
    def _():
        mine.start()

    @pl.when(jnp.logical_not(stays))
    def _():
        theirs.start()

    return mine


def feed_grads(flat, back_refs, mine_ref, theirs_ref, held, sems):
    rows_ref, inner_ref, dgate_ref, dup_ref, df_ref, da_ref = back_refs
    rows = rows_ref[...].astype(F32).T.astype(BF)
    flat = flat.astype(F32).T.astype(BF)
    df = df_ref[...].astype(F32).T.astype(BF)
    copies = []

    def sent(j):
        for r in range(2):
            copies.append(send_chunk(held, mine_ref, theirs_ref, sems, r * 16 + j))

    def put(value, j):
        for half in range(2):
            for r in range(2):
                at = half * HALF + r * QUARTER
                held[r * 16 + j, half] = value[at : at + QUARTER].astype(BF)
        sent(j)

    empty = jnp.zeros((QUARTER, LANES), BF)
    for j in (14, 15):
        for half in range(2):
            for r in range(2):
                held[r * 16 + j, half] = empty
        sent(j)
    for j in range(4):
        lanes = slice(j * LANES, (j + 1) * LANES)
        put(nn(rows, dgate_ref[:, lanes]), j)
        put(nn(rows, dup_ref[:, lanes]), 4 + j)
    for j in range(2):
        for half in range(2):
            at = half * (FF // 2) + j * LANES
            value = nn(df, inner_ref[:, at : at + LANES])
            for top in range(2):
                for r in range(2):
                    line = top * HALF + r * QUARTER
                    held[r * 16 + 8 + 2 * top + j, half] = value[line : line + QUARTER].astype(BF)
        sent(8 + j)
        sent(10 + j)
    put(nn(flat, da_ref[:, :LANES]), 12)
    put(nn(flat, da_ref[:, LANES:]), 13)
    return copies


def second_kernel(*refs):
    kv_refs, refs = refs[:PIECES], refs[PIECES:]
    (x_ref, cot_ref, query_ref, bias_ref, tri_ref, cos_ref, sin_ref), refs = refs[:7], refs[7:]
    a, b, refs = refs[:7], refs[7:14], refs[14:]
    (act_ref, dh2_ref, dq_ref, gain_ref), refs = refs[:4], refs[4:]
    dkv_refs, grads_refs, refs = refs[:PIECES], refs[PIECES : PIECES + 2], refs[PIECES + 2 :]
    a_scr, b_scr, back_refs, held = refs[:3], refs[3:5], refs[5:11], refs[11:]
    copies_b = fetch_b(1, b, *b_scr)
    copies_a = fetch_a(1, a, *a_scr)
    bias, triangle = bias_ref[...], tri_ref[...]
    mixed, logs = attend(query_ref, kv_refs, bias, triangle)
    wait_all(copies_b + copies_a)
    w_gate, w_up, w_down, w_out = b_values(b_scr[0])
    flat = ungroup([m.astype(F32) for m in mixed]).T.astype(BF)
    middle = read_turned(x_ref) + nn(flat, w_out)
    gain = gain_rows(a_scr[1])[1]
    parts = feed(middle, gain, w_gate, w_up)
    dh2, do = feed_back(
        read_turned(cot_ref), middle, gain, w_gate, w_up, w_down, w_out, parts, (*back_refs, gain_ref)
    )
    copies = feed_grads(flat, back_refs, *grads_refs, *held)
    act_ref[...] = (middle + down(back_refs[1][...], w_down)).T.astype(BF)
    dh2_ref[...] = dh2
    dq = attend_back(query_ref, kv_refs, bias, triangle, mixed, logs, do, dkv_refs)
    dq_ref[...] = query_back(dq, cos_ref[...], sin_ref[...])
    wait_all(copies)


def third_kernel(*refs):
    kv_refs, refs = refs[:PIECES], refs[PIECES:]
    own_dkv, refs = refs[:4], refs[4:]
    (act_ref, dh2_ref, dq_ref, mixed_ref, logs_ref, middle_ref, query_ref), refs = refs[:7], refs[7:]
    (bias_ref, tri_ref, cos_ref, sin_ref), refs = refs[:4], refs[4:]
    a, b, refs = refs[:7], refs[7:14], refs[14:]
    (grad1_ref, rows1_ref, dqkv1_ref, gain1_ref), refs = refs[:4], refs[4:]
    (dh2_out_ref, dq_out_ref, gain_ref), refs = refs[:3], refs[3:]
    dkv_refs, grads_refs, refs = refs[:PIECES], refs[PIECES : PIECES + 2], refs[PIECES + 2 :]
    a_scr, a0_scr, b_scr, back_refs, held = refs[:3], refs[3:6], refs[6:8], refs[8:14], refs[14:]
    copies_a = fetch_a(1, a, *a_scr)
    copies_a0 = fetch_a(0, a, *a0_scr)
    copies_b = fetch_b(0, b, *b_scr)
    cosine, sine = cos_ref[...], sin_ref[...]
    wait_all(copies_a)
    grad = entry_back(
        read_turned(act_ref), gain_rows(a_scr[1])[0], a_scr[0][...], cosine, sine,
        dq_ref[...], own_dkv, dh2_ref[...], rows1_ref, dqkv1_ref, gain1_ref,
    )
    grad1_ref[...] = grad.T
    wait_all(copies_a0 + copies_b)
    w_gate, w_up, w_down, w_out = b_values(b_scr[0])
    mixed = [mixed_ref[g] for g in range(KV_HEADS)]
    logs = [logs_ref[g : g + 1] for g in range(KV_HEADS)]
    flat = ungroup([m.astype(F32) for m in mixed]).T.astype(BF)
    gain = gain_rows(a0_scr[1])[1]
    middle = middle_ref[...]
    parts = feed(middle, gain, w_gate, w_up)
    dh2, do = feed_back(
        grad.astype(BF).astype(F32), middle, gain, w_gate, w_up, w_down, w_out, parts, (*back_refs, gain_ref)
    )
    copies_g = feed_grads(flat, back_refs, *grads_refs, *held)
    dh2_out_ref[...] = dh2
    dq = attend_back(query_ref, kv_refs, bias_ref[...], tri_ref[...], mixed, logs, do, dkv_refs)
    dq_out_ref[...] = query_back(dq, cosine, sine)
    wait_all(copies_g)


def close_kernel(*refs):
    own_dkv, refs = refs[:4], refs[4:]
    (x_ref, dh2_ref, dq_ref, cos_ref, sin_ref), refs = refs[:5], refs[5:]
    a, refs = refs[:7], refs[7:]
    (grad_ref, rows_ref, dqkv_ref, gain_ref), a_scr = refs[:4], refs[4:]
    copies = fetch_a(0, a, *a_scr)
    wait_all(copies)
    grad = entry_back(
        read_turned(x_ref), gain_rows(a_scr[1])[0], a_scr[0][...], cos_ref[...], sin_ref[...],
        dq_ref[...], own_dkv, dh2_ref[...], rows_ref, dqkv_ref, gain_ref,
    )
    grad_ref[...] = grad.T


def entry_grads_kernel(*refs):
    mine_ref, theirs_ref = refs[8:]
    values = []
    for layer in range(2):
        rows_ref, dqkv_ref, gain_attn_ref, gain_mlp_ref = refs[4 * layer : 4 * layer + 4]
        rows = rows_ref[...].astype(F32).T.astype(BF)
        value = nn(rows, dqkv_ref[...])
        gains = jnp.concatenate(
            [gain_attn_ref[...], gain_mlp_ref[...], jnp.zeros((HEAD_DIM - 2, D), F32)], 0
        ).T
        values.append(jnp.concatenate([value, gains], 1).astype(BF))
    for r in range(2):
        for j in range(16):
            lanes = slice(j * HEAD_DIM, (j + 1) * HEAD_DIM)
            parts = [
                value[half * HALF + r * QUARTER : half * HALF + (r + 1) * QUARTER, lanes]
                for value in values
                for half in range(2)
            ]
            put_chunk(mine_ref, theirs_ref, r * 16 + j, jnp.concatenate(parts, 1))


def merge_kernel(*refs):
    feeds, entries, early, merged = refs[:4], refs[4:8], refs[8:12], refs[12:]
    for k in range(4):
        feed0 = sum(part[k].astype(F32) for part in feeds)
        entry = sum(part[k].astype(F32) for part in entries)
        for layer in range(2):
            for half in range(2):
                at = 2 * layer + half
                block = feed0[half].astype(BF) if layer == 0 else early[k][half]
                merged[k][at, :, :LANES] = block
                merged[k][at, :, LANES:] = entry[:, at * HEAD_DIM : (at + 1) * HEAD_DIM].astype(BF)


def unpack_kernel(*refs):
    came, refs = refs[:8], refs[8:]
    (norms_ref, query_ref, key_ref, value_ref, out_ref, gate_ref, up_ref, down_ref), (held,) = refs[:8], refs[8:]
    y, x, core = here()
    for piece in range(8):
        which = core if piece < 4 else 1 - core
        k2 = piece % 4
        for k1 in range(4):
            back_y = jnp.where(which == 0, k1, k2)
            back_x = jnp.where(which == 0, k2, k1)
            chunk = lax.rem(y + 4 - back_y, 4) * 8 + lax.rem(x + 4 - back_x, 4) * 2 + which
            held[chunk] = came[piece][k1]
    for r in range(2):
        rows = slice(r * QUARTER, (r + 1) * QUARTER)

        def block(j):
            return held[r * 16 + j, :, :LANES].astype(F32)

        def head(j):
            return held[r * 16 + j, :, LANES:].astype(F32)

        for j in range(4):
            lanes = slice(j * LANES, (j + 1) * LANES)
            gate_ref[rows, lanes] = block(j)
            up_ref[rows, lanes] = block(4 + j)
        for j in range(2):
            lanes = slice(j * LANES, (j + 1) * LANES)
            for top in range(2):
                down_ref[top * HALF + r * QUARTER : top * HALF + (r + 1) * QUARTER, lanes] = block(8 + 2 * top + j)
        out_ref[rows] = jnp.concatenate([block(12), block(13)[:, : D - LANES]], 1)
        query_ref[rows] = jnp.concatenate([head(j) for j in range(HEADS)], 1)
        key_ref[rows] = jnp.concatenate([head(HEADS + j) for j in range(KV_HEADS)], 1)
        value_ref[rows] = jnp.concatenate([head(HEADS + KV_HEADS + j) for j in range(KV_HEADS)], 1)
    turned = jnp.concatenate([held[r * 16 + 15, :, LANES:].astype(F32).T for r in range(2)], 1)
    norms_ref[...] = turned[:8]


def routes(axes_size):
    def turn_of(i, along_y, k):
        core, x, y = i % 2, i // 2 % 4, i // 8
        if along_y:
            y = (y + k) % 4
        else:
            x = (x + k) % 4
        return y * 8 + x * 2 + core

    def first(k):
        return [(i, turn_of(i, i % 2 == 0, k)) for i in range(axes_size)]

    def second(k):
        return [(i, turn_of(i, i % 2 == 1, k)) for i in range(axes_size)]

    return first, second, [(i, i ^ 1) for i in range(axes_size)]


def per_device(
    inputs, cotangent, positions, norm_attn, w_query, w_key, w_value, w_out, norm_mlp, w_gate, w_up, w_down
):
    section = lax.axis_index("section")
    place = lax.axis_index("ctx")
    core = place % 2
    first, second, swap = routes(lax.axis_size("ctx"))

    def hop(block, route):
        return lax.ppermute(block, "ctx", route)

    def along_z(block, flip):
        return lax.ppermute(block, ("section", "wsh"), [(i, i ^ flip) for i in range(4)])

    spots = lax.dynamic_index_in_dim(positions, section, 0, keepdims=False)[0]
    gains = jnp.concatenate(
        [norm_attn, jnp.zeros((1, 96), BF), norm_mlp, jnp.zeros((1, A_WIDTH - 384 - HALF), BF)], 1
    )
    gains = jnp.concatenate([gains, jnp.zeros((15, A_WIDTH), BF)], 0)
    own_a = jnp.concatenate([w_query[0], w_key[0], w_value[0]], 1)
    half_a = jnp.concatenate([lax.dynamic_slice_in_dim(own_a, core * QUARTER, QUARTER, 0), gains], 0)
    own_a = jnp.concatenate([own_a, gains], 0)
    turned = w_down[0].T
    parts_b = [w_gate[0], w_up[0], turned[:HALF], turned[HALF:], w_out[0]]
    spare = B_WIDTH - OUT_AT - D
    own_b = jnp.concatenate(parts_b + [jnp.zeros((HALF, spare), BF)], 1)
    parts_b = [lax.dynamic_slice_in_dim(part, core * QUARTER, QUARTER, 0) for part in parts_b]
    half_b = jnp.concatenate(parts_b + [jnp.zeros((QUARTER, spare), BF)], 1)

    y, x_at = place // 8, place // 2 % 4
    ring_place = jnp.where(core == 0, y, x_at)
    part = along_z(lax.dynamic_slice_in_dim(half_b, ring_place * B_PART, B_PART, 1), 1)
    came = [along_z(half_a, flip) for flip in (2, 1, 3)]
    a = [own_a] + came + [hop(block, swap) for block in came]

    x = lax.dynamic_index_in_dim(inputs, section, 0, keepdims=False)[0].T
    cot = lax.dynamic_index_in_dim(cotangent, section, 0, keepdims=False)[0].T
    freq = BASE ** (-(jnp.arange(HEAD_DIM // 2, dtype=F32) * 2.0 / HEAD_DIM))
    angle = freq[:, None] * spots.astype(F32)[None, :]
    cosine, sine = jnp.cos(angle), jnp.sin(angle)
    triangle = jnp.where(spots[:, None] <= spots[None, :], 0.0, NEG).astype(F32)

    run_of = spots // RUN
    runs_mine = jnp.concatenate([run_of[:1], run_of[RUN : RUN + 1], jnp.zeros((14,), jnp.int32)])
    runs_mine = jnp.broadcast_to(runs_mine[:, None], (16, KVW)).astype(BF)
    runs_query = jnp.tile(run_of, GROUP).astype(F32)[None]

    def gathered(own):
        four = jnp.concatenate([own] + [hop(own, first(k)) for k in (1, 2, 3)], 0)
        mine = [four] + [hop(four, second(k)) for k in (1, 2, 3)]
        return mine + [hop(piece, swap) for piece in mine]

    def summed(pieces):
        mine = [add(pieces[k], hop(pieces[4 + k], swap)) for k in range(4)]
        four = add(mine[0], *[hop(mine[k], second(-k)) for k in (1, 2, 3)])
        parts = [four[k * SPAN : (k + 1) * SPAN] for k in range(4)]
        return [parts[0]] + [hop(parts[k], first(-k)) for k in (1, 2, 3)]

    def add(*parts):
        return sum(part.astype(F32) for part in parts).astype(BF)

    half_b, *_ = lax.optimization_barrier((half_b, *came))
    near, across = along_z(half_b, 2), along_z(half_b, 3)
    query0, own0 = call(
        open_kernel, [(VM, [x, cosine, sine, runs_mine]), (HBM, a)], [QUERY, shape((MARKED, KVW))], A_SCRATCH, 10**8
    )
    all0 = gathered(own0)
    part, *_ = lax.optimization_barrier((part, *all0[1:4]))
    far = [part] + [hop(part, first(k)) for k in (1, 2, 3)]
    mixed0, logs0, bias = call(
        mix_kernel,
        [(VM, all0 + [query0, runs_query, triangle])],
        [MIXED, LOGS, shape((RUNS, ROWS))],
        [],
        10**9,
    )
    mixed0, near, across, *far = lax.optimization_barrier((mixed0, near, across, *far))
    far = jnp.stack(far)
    b = [own_b, near, far, across] + [hop(block, swap) for block in (near, far, across)]
    act0, middle0, query1, own1 = call(
        first_kernel,
        [(VM, [x, mixed0, cosine, sine]), (HBM, a + b)],
        [TURNED, TOKENS32, QUERY, OWN],
        A_SCRATCH + A_SCRATCH + B_SCRATCH,
        10**9,
    )
    all1 = gathered(own1)
    act1, dh2, dq, gain_mlp1, *rest = call(
        second_kernel,
        [(VM, all1 + [act0, cot, query1, bias, triangle, cosine, sine]), (HBM, a + b)],
        [TURNED, TOKENS32, TOKENS, GAIN] + [PIECE] * PIECES + FEEDS,
        A_SCRATCH + B_SCRATCH + GRAD_SCRATCH,
        7 * 10**9,
        2,
    )
    dkv, feed1 = rest[:PIECES], rest[PIECES:]

    def exchanged(own, other):
        kept = jnp.where(section == 0, own, other)
        sent = jnp.where(section == 0, other, own)
        came = lax.ppermute(sent, "section", [(0, 1), (1, 0)])
        return jnp.where(section == 0, jnp.stack([kept, came]), jnp.stack([came, kept]))

    def to_cores(mine, theirs):
        came = hop(theirs, swap)
        return [add(mine[4 * k : 4 * k + 4], came[4 * k : 4 * k + 4]) for k in range(4)]

    def to_rings(sets):
        return [sets[0]] + [hop(sets[k], second(-k)) for k in (1, 2, 3)]

    ENTRIES = [shape((16, QUARTER, 4 * HEAD_DIM))] * 2
    own_dkv = summed(dkv)
    feed1 = to_cores(*feed1)
    acts = exchanged(act0, act1)
    dq, acts, *feed1 = lax.optimization_barrier((dq, acts, *feed1))
    feed1, _ = lax.optimization_barrier((feed1, own_dkv))
    feed1 = to_rings(feed1)
    (
        grad1, rows_in1, dqkv1, gain_attn1,
        dh2, dq, gain_mlp0, *rest,
    ) = call(
        third_kernel,
        [
            (VM, all0 + own_dkv + [act0, dh2, dq, mixed0, logs0, middle0, query0]),
            (VM, [bias, triangle, cosine, sine]),
            (HBM, a + b),
        ],
        [TURNED32, TOKENS, shape((SPAN, QKV)), GAIN]
        + [TOKENS32, TOKENS, GAIN]
        + [PIECE] * PIECES
        + FEEDS,
        A_SCRATCH + A_SCRATCH + B_SCRATCH + GRAD_SCRATCH,
        6 * 10**9,
        2,
    )
    (grad1, rows_in1, dqkv1, gain_attn1, dh2, dq, gain_mlp0, rest, feed1) = lax.optimization_barrier(
        (grad1, rows_in1, dqkv1, gain_attn1, dh2, dq, gain_mlp0, rest, feed1)
    )
    dkv, feed0 = rest[:PIECES], rest[PIECES:]
    own_dkv = summed(dkv)
    feed0 = to_cores(*feed0)
    early = [add(*[block[k] for block in feed1]) for k in range(4)]
    *own_dkv, feed0, early = lax.optimization_barrier((*own_dkv, feed0, early))
    feed0 = to_rings(feed0)
    grad0, rows_in0, dqkv0, gain_attn0 = call(
        close_kernel,
        [(VM, own_dkv + [x, dh2, dq, cosine, sine]), (HBM, a)],
        [TURNED32, TOKENS, shape((SPAN, QKV)), GAIN],
        A_SCRATCH,
        10**8,
    )
    entries = call(
        entry_grads_kernel,
        [(VM, [rows_in0, dqkv0, gain_attn0, gain_mlp0, rows_in1, dqkv1, gain_attn1, gain_mlp1])],
        ENTRIES,
        [],
        10**8,
    )
    entries, feed0 = lax.optimization_barrier((list(entries), feed0))
    entries = to_rings(to_cores(*entries))
    grads = exchanged(grad0, grad1)
    merged = call(
        merge_kernel, [(VM, feed0 + entries + early)], [shape((4, QUARTER, LANES + HEAD_DIM))] * 4, [], 10**8
    )

    every = add(merged[0], *[hop(merged[k], first(-k)) for k in (1, 2, 3)])
    spot = section * 2 + lax.axis_index("wsh")

    def chunk(flip):
        return lax.dynamic_index_in_dim(every, spot ^ flip, 0, keepdims=False)

    total = add(chunk(0), *[along_z(chunk(flip), flip) for flip in (1, 2, 3)])
    four = jnp.stack([total] + [hop(total, first(k)) for k in (1, 2, 3)])
    mine = [four] + [hop(four, second(k)) for k in (1, 2, 3)]
    mine[1], grads = lax.optimization_barrier((mine[1], grads))
    came = mine + [hop(piece, swap) for piece in mine]
    norms, g_query, g_key, g_value, g_out, g_gate, g_up, g_down = call(
        unpack_kernel,
        [(VM, came)],
        [
            shape((8, HALF), F32), shape((HALF, D), F32), shape((HALF, KVW // 2), F32), shape((HALF, KVW // 2), F32),
            shape((HALF, D), F32), shape((HALF, FF), F32), shape((HALF, FF), F32), shape((D, FF // 2), F32),
        ],
        [pltpu.VMEM((CHUNKS, QUARTER, LANES + HEAD_DIM), BF)],
        10**8,
    )

    return (
        acts.swapaxes(1, 2)[None, :, None],
        grads.swapaxes(1, 2)[None, :, None],
        norms[0:1],
        g_query[None],
        g_key[None],
        g_value[None],
        g_out[None],
        norms[1:2],
        g_gate[None],
        g_up[None],
        g_down.T[None],
    )


def solution(mesh):
    placed = (
        P(None, "wsh", "ctx", None),
        P(None, "wsh", "ctx", None),
        P(None, "wsh", "ctx"),
        P("section", "wsh"),
        P("section", "wsh", None),
        P("section", "wsh", None),
        P("section", "wsh", None),
        P("section", "wsh", None),
        P("section", "wsh"),
        P("section", "wsh", None),
        P("section", "wsh", None),
        P("section", "wsh", None),
    )
    return jax.shard_map(
        per_device,
        mesh=mesh,
        in_specs=placed,
        out_specs=(
            P("section", None, "wsh", "ctx", None),
            P("section", None, "wsh", "ctx", None),
            P("section", "wsh"),
            P("section", "wsh", None),
            P("section", "wsh", None),
            P("section", "wsh", None),
            P("section", "wsh", None),
            P("section", "wsh"),
            P("section", "wsh", None),
            P("section", "wsh", None),
            P("section", "wsh", None),
        ),
        check_vma=False,
    )
```

```python
import jax
import jax.numpy as jnp
from jax import lax
from jax.experimental import pallas as pl
from jax.experimental.pallas import tpu as pltpu
from jax.sharding import PartitionSpec as P

HEADS = 9
KV_HEADS = 3
GROUP = HEADS // KV_HEADS
HEAD_DIM = 64
D = HEADS * HEAD_DIM
FF = 1536
QKV = D + 2 * KV_HEADS * HEAD_DIM
KVW = 2 * KV_HEADS * HEAD_DIM
SPAN = 128
RUN = 64
LENGTH = 4096
RUNS = LENGTH // RUN
ROWS = GROUP * SPAN
BLOCK = 512
PIECES = LENGTH // BLOCK
PER_PIECE = BLOCK // SPAN
MARKED = SPAN + 16

EPS = 1e-05
NEG = -1e30
BASE = 100000.0
SCALE = HEAD_DIM ** (-0.5)

BF = jnp.bfloat16
F32 = jnp.float32
VMEM_LIMIT = 56 * 1024 * 1024


def nn(left, right):
    return lax.dot_general(left, right, (((1,), (0,)), ((), ())), preferred_element_type=F32)


def nt(left, right):
    return lax.dot_general(left, right, (((1,), (1,)), ((), ())), preferred_element_type=F32)


def normalize(hidden):
    inverse = lax.rsqrt(jnp.mean(hidden * hidden, -1, keepdims=True) + EPS)
    return hidden * inverse, inverse


def norm_back(grad, normed, inverse):
    return inverse * (grad - normed * jnp.mean(grad * normed, -1, keepdims=True))


def turn(head, cosine, sine):
    half = HEAD_DIM // 2
    first, second = head[:half], head[half:]
    return jnp.concatenate([first * cosine - second * sine, second * cosine + first * sine], 0)


def turn_back(head, cosine, sine):
    half = HEAD_DIM // 2
    first, second = head[:half], head[half:]
    return jnp.concatenate([first * cosine + second * sine, second * cosine - first * sine], 0)


def head_rows(array, head):
    return array[head * HEAD_DIM : (head + 1) * HEAD_DIM]


def group_of(array, group):
    return jnp.concatenate([head_rows(array, group * GROUP + r) for r in range(GROUP)], 1)


def ungroup(parts):
    return jnp.concatenate(
        [parts[g][:, r * SPAN : (r + 1) * SPAN] for g in range(KV_HEADS) for r in range(GROUP)], 0
    )


def attn_rows(hidden, gain):
    normed, inverse = normalize(hidden)
    return normed, inverse, (normed * gain).astype(BF)


def project(rows, w_qkv, cosine, sine, query_ref, kv_ref):
    flat = nn(rows, w_qkv).T
    heads = [turn(head_rows(flat, j), cosine, sine) * SCALE for j in range(HEADS)]
    for g in range(KV_HEADS):
        query_ref[g] = jnp.concatenate(heads[g * GROUP : (g + 1) * GROUP], 1).astype(BF)
    parts = []
    for g in range(KV_HEADS):
        parts.append(turn(head_rows(flat, HEADS + g), cosine, sine))
        parts.append(head_rows(flat, HEADS + KV_HEADS + g))
    kv_ref[...] = jnp.concatenate(parts, 0).T.astype(BF)


def one_hot(first_run, rows):
    lane = lax.broadcasted_iota(jnp.int32, (rows, SPAN), 1)
    run = lax.broadcasted_iota(jnp.int32, (rows, SPAN), 0) // RUN + first_run
    marked = (lane == run) | ((lane >= RUNS) & (lane < RUNS + 3))
    return jnp.where(marked, 1.0, 0.0).astype(BF)


def columns(g):
    return slice(g * SPAN, (g + 1) * SPAN)


def key_rows(piece, skip, g):
    if piece.shape[0] == BLOCK:
        return piece[skip:, columns(g)]
    first = skip // SPAN
    return jnp.concatenate(
        [piece[k * MARKED : k * MARKED + SPAN, columns(g)] for k in range(first, PER_PIECE)], 0
    )


def attend(query_ref, kv_refs, bias, triangle):
    zeros = jnp.zeros((HEAD_DIM, ROWS), BF)
    fixed = [jnp.concatenate([query_ref[g], zeros, bias, zeros], 0) for g in range(KV_HEADS)]
    triangle = jnp.concatenate([triangle] * GROUP, 1)
    start = []
    for g in range(KV_HEADS):
        own = kv_refs[0][:SPAN, columns(g)]
        scores = nn(own, fixed[g][:SPAN]) + triangle
        top = jnp.max(scores, 0, keepdims=True)
        probs = jnp.exp(scores - top)
        start += [top, jnp.sum(probs, 0, keepdims=True), nn(own.T[HEAD_DIM:], probs.astype(BF))]

    def step(b, carry):
        skip = SPAN if b == 0 else 0
        marks = one_hot((b * BLOCK + skip) // RUN, BLOCK - skip)
        out = []
        for g in range(KV_HEADS):
            top, total, accum = carry[3 * g : 3 * g + 3]
            block = key_rows(kv_refs[b], skip, g)
            scores = nn(jnp.concatenate([block, marks], 1), fixed[g])
            higher = jnp.maximum(top, jnp.max(scores, 0, keepdims=True))
            probs = jnp.exp(scores - higher)
            fade = jnp.exp(top - higher)
            total = total * fade + jnp.sum(probs, 0, keepdims=True)
            accum = accum * fade + nn(block.T[HEAD_DIM:], probs.astype(BF))
            out += [higher, total, accum]
        return tuple(out)

    done = tuple(start)
    for b in range(PIECES):
        done = step(b, done)
    mixed = [(done[3 * g + 2] / done[3 * g + 1]).astype(BF) for g in range(KV_HEADS)]
    logs = [done[3 * g] + jnp.log(done[3 * g + 1]) for g in range(KV_HEADS)]
    return mixed, logs


def attend_back(query_ref, kv_refs, bias, triangle, mixed, logs, mixed_grad, dkv_refs):
    zeros = jnp.zeros((HEAD_DIM, ROWS), BF)
    row = lax.broadcasted_iota(jnp.int32, (HEAD_DIM, 2 * ROWS), 0)
    triangle = jnp.concatenate([triangle] * GROUP, 1)
    fixed, turned = [], []
    for g in range(KV_HEADS):
        grads = group_of(mixed_grad, g)
        delta = jnp.sum(grads.astype(F32) * mixed[g].astype(F32), 0, keepdims=True)
        less = -jnp.concatenate([logs[g], delta], 1)
        high = less.astype(BF).astype(F32)
        middle = (less - high).astype(BF).astype(F32)
        lowest = less - high - middle
        stats = jnp.where(row == 0, high, jnp.where(row == 1, middle, jnp.where(row == 2, lowest, 0.0)))
        both = jnp.concatenate(
            [jnp.concatenate([query_ref[g], zeros], 1), jnp.concatenate([zeros, grads], 1)], 0
        )
        fixed.append(
            jnp.concatenate([both, jnp.concatenate([bias, zeros], 1), stats.astype(BF)], 0)
        )
        turned.append(both.T)

    def terms(block, marks, g, extra):
        both = nn(jnp.concatenate([block, marks], 1), fixed[g])
        scores = both[:, :ROWS]
        if extra is not None:
            scores = scores + extra
        probs = jnp.exp(scores)
        score_grad = (probs * both[:, ROWS:]).astype(BF)
        kv_terms = nn(jnp.concatenate([score_grad, probs.astype(BF)], 1), turned[g])
        return kv_terms.astype(BF), nn(block.T[:HEAD_DIM], score_grad)

    sums = [jnp.zeros((HEAD_DIM, ROWS), F32)] * KV_HEADS
    for b in range(PIECES):
        skip = SPAN if b == 0 else 0
        marks = one_hot((b * BLOCK + skip) // RUN, BLOCK - skip)
        for g in range(KV_HEADS):
            kv_terms, query_terms = terms(key_rows(kv_refs[b], skip, g), marks, g, None)
            dkv_refs[b][skip:, columns(g)] = kv_terms
            sums[g] = sums[g] + query_terms
    marks = one_hot(2 * RUNS, SPAN)
    for g in range(KV_HEADS):
        kv_terms, query_terms = terms(kv_refs[0][:SPAN, columns(g)], marks, g, triangle)
        dkv_refs[0][:SPAN, columns(g)] = kv_terms
        sums[g] = sums[g] + query_terms
    return ungroup(sums) * SCALE


def feed(middle, gain, w_gate, w_up):
    normed, inverse = normalize(middle)
    rows = (normed * gain).astype(BF)
    return normed, inverse, rows, nn(rows, w_gate), nn(rows, w_up)


def down(inner, w_down):
    half = FF // 2
    return nt(inner[:, :half], w_down[0]) + nt(inner[:, half:], w_down[1])


def feed_back(outgrad, middle, gain, w_gate, w_up, w_down, w_out, parts, refs):
    normed, inverse, rows, gate, upper = parts
    rows_ref, inner_ref, dgate_ref, dup_ref, df_ref, da_ref, gain_ref = refs
    sigma = jax.nn.sigmoid(gate)
    swish = gate * sigma
    df = outgrad.astype(BF)
    inner_grad = jnp.concatenate([nn(df, w_down[i]) for i in range(2)], 1)
    gate_grad = (inner_grad * upper * sigma * (1.0 + gate * (1.0 - sigma))).astype(BF)
    up_grad = (inner_grad * swish).astype(BF)
    rows_grad = nt(gate_grad, w_gate) + nt(up_grad, w_up)
    gain_ref[...] = jnp.sum(rows_grad * normed, 0, keepdims=True)
    middle_grad = outgrad + norm_back(rows_grad * gain, normed, inverse)
    da = middle_grad.astype(BF)
    rows_ref[...] = rows
    inner_ref[...] = (swish * upper).astype(BF)
    dgate_ref[...] = gate_grad
    dup_ref[...] = up_grad
    df_ref[...] = df
    da_ref[:, :D] = da
    da_ref[:, D:] = jnp.zeros((SPAN, 2 * LANES - D), BF)
    return middle_grad, nt(da, w_out).T.astype(BF)


def query_back(dq, cosine, sine):
    parts = [turn_back(head_rows(dq, j), cosine, sine) for j in range(HEADS)]
    return jnp.concatenate(parts, 0).T.astype(BF)


def entry_back(hidden, gain, w_qkv, cosine, sine, query_grad, dkv, middle_grad, rows_ref, dqkv_ref, gain_ref):
    turned = sum(part[...].astype(F32) for part in dkv).T
    parts = [turn_back(head_rows(turned, 2 * g), cosine, sine) for g in range(KV_HEADS)]
    parts += [head_rows(turned, 2 * g + 1) for g in range(KV_HEADS)]
    kv_grad = jnp.concatenate(parts, 0).T.astype(BF)
    grads = jnp.concatenate([query_grad.astype(F32), kv_grad.astype(F32)], 1).astype(BF)
    normed, inverse, rows = attn_rows(hidden, gain)
    rows_grad = nt(grads, w_qkv)
    rows_ref[...] = rows
    dqkv_ref[...] = grads
    gain_ref[...] = jnp.sum(rows_grad * normed, 0, keepdims=True)
    return middle_grad + norm_back(rows_grad * gain, normed, inverse)


VM = pl.BlockSpec(memory_space=pltpu.VMEM)
HBM = pl.BlockSpec(memory_space=pl.ANY)
HALF = D // 2
QUARTER = HALF // 2
A_WIDTH = QKV
B_PART = 1408
B_WIDTH = 4 * B_PART
DOWN_AT = 2 * FF
OUT_AT = 3 * FF


def shape(dims, kind=BF):
    return jax.ShapeDtypeStruct(dims, kind)


def here():
    place = lax.axis_index("ctx")
    return place // 8, lax.rem(place // 2, 4), lax.rem(place, 2)


def start_quarters(layer, sources, copies_of, far_copies_of):
    own, near, far, across, near_twin, far_twin, across_twin = sources
    section, half = lax.axis_index("section"), lax.axis_index("wsh")
    core = here()[2]
    home, away = [], []
    for m, place in enumerate((core, 1 - core)):
        home += copies_of(own, place * QUARTER, True, half, place, m)
        home += far_copies_of(far_twin if m else far, 1 - half, place, 2 + m)
        away += copies_of(near_twin if m else near, 0, False, half, place, m)
        away += copies_of(across_twin if m else across, 0, False, 1 - half, place, 2 + m)

    @pl.when(section == layer)
    def _():
        for copy in home:
            copy.start()

    @pl.when(section != layer)
    def _():
        for copy in away:
            copy.start()

    return away


def rows_at(start, size):
    if isinstance(start, int):
        return pl.ds(start, size)
    return pl.ds(pl.multiple_of(start, 16), size)


def fetch_a(layer, sources, matrix, gains, sems):
    def copies_of(source, first, whole, rows, place, k):
        gain_at = HALF if whole else QUARTER
        out = [
            pltpu.make_async_copy(
                source.at[rows_at(first, QUARTER)],
                matrix.at[rows_at(rows * HALF + place * QUARTER, QUARTER)],
                sems.at[k],
            )
        ]
        if k % 2 == 0:
            out.append(
                pltpu.make_async_copy(
                    source.at[rows_at(gain_at, 16)], gains.at[rows_at(rows * 16, 16)], sems.at[4 + k // 2]
                )
            )
        return out

    def far_copies_of(source, rows, place, k):
        return copies_of(source, 0, False, rows, place, k)

    return start_quarters(layer, sources, copies_of, far_copies_of)


def gain_rows(gains):
    values = gains[...].astype(F32)
    return [
        jnp.concatenate([values[0:1, at : at + HALF], values[16:17, at : at + HALF]], 1) for at in (0, 384)
    ]


def fetch_b(layer, sources, matrix, sems):
    y, x, core = here()

    def copies_of(source, first, whole, rows, place, k):
        return [
            pltpu.make_async_copy(
                source.at[rows_at(first, QUARTER)],
                matrix.at[rows_at(rows * HALF + place * QUARTER, QUARTER)],
                sems.at[k],
            )
        ]

    def far_copies_of(source, rows, place, k):
        at = jnp.where(place == 0, y, x)
        return [
            pltpu.make_async_copy(
                source.at[back],
                matrix.at[
                    rows_at(rows * HALF + place * QUARTER, QUARTER),
                    pl.ds(pl.multiple_of(lax.rem(at + 4 - back, 4) * B_PART, 128), B_PART),
                ],
                sems.at[k],
            )
            for back in range(4)
        ]

    return start_quarters(layer, sources, copies_of, far_copies_of)


def wait_all(copies):
    for copy in copies:
        copy.wait()


A_SCRATCH = [pltpu.VMEM((D, A_WIDTH), BF), pltpu.VMEM((32, A_WIDTH), BF), pltpu.SemaphoreType.DMA((6,))]
B_SCRATCH = [pltpu.VMEM((D, B_WIDTH), BF), pltpu.SemaphoreType.DMA((4,))]


def b_values(matrix):
    halves = [
        jnp.concatenate([matrix[low : low + HALF, at : at + FF // 2] for at in (DOWN_AT, DOWN_AT + FF // 2)], 0)
        for low in (0, HALF)
    ]
    return matrix[:, :FF], matrix[:, FF : 2 * FF], halves, matrix[:, OUT_AT : OUT_AT + D]


def call(kernel, ins, out_shape, scratch, flops, in_hbm=0):
    specs = [spec for spec, arrays in ins for _ in arrays]
    arrays = [array for _, arrays in ins for array in arrays]
    return pl.pallas_call(
        kernel,
        in_specs=specs,
        out_specs=[VM] * (len(out_shape) - in_hbm) + [HBM] * in_hbm,
        out_shape=out_shape,
        scratch_shapes=scratch,
        compiler_params=pltpu.CompilerParams(vmem_limit_bytes=VMEM_LIMIT),
        cost_estimate=pl.CostEstimate(flops=flops // 1000, bytes_accessed=10_000, transcendentals=0),
    )(*arrays)


QUERY = shape((KV_HEADS, HEAD_DIM, ROWS))
OWN = shape((SPAN, KVW))
TOKENS = shape((SPAN, D))
TURNED = shape((D, SPAN))
TURNED32 = shape((D, SPAN), F32)
TOKENS32 = shape((SPAN, D), F32)
MIXED = shape((KV_HEADS, HEAD_DIM, ROWS))
LOGS = shape((8, ROWS), F32)
GAIN = shape((1, D), F32)
WIDE = shape((SPAN, FF))
GRAD_SCRATCH = [
    pltpu.VMEM((SPAN, D), BF),
    pltpu.VMEM((SPAN, FF), BF),
    pltpu.VMEM((SPAN, FF), BF),
    pltpu.VMEM((SPAN, FF), BF),
    pltpu.VMEM((SPAN, D), BF),
    pltpu.VMEM((SPAN, 768), BF),
    pltpu.VMEM((32, 2, QUARTER, 384), BF),
    pltpu.SemaphoreType.DMA((32,)),
]
FEEDS = [shape((16, 2, QUARTER, 384))] * 2
PIECE = shape((BLOCK, KVW))


def read_turned(ref):
    return ref[...].astype(F32).T


def open_kernel(x_ref, cos_ref, sin_ref, runs_ref, *refs):
    a, (query_ref, kv_ref), (wqkv, gains, sems) = refs[:7], refs[7:9], refs[9:]
    copies = fetch_a(0, a, wqkv, gains, sems)
    cosine, sine = cos_ref[...], sin_ref[...]
    normed, _ = normalize(read_turned(x_ref))
    kv_ref[SPAN:] = runs_ref[...]
    wait_all(copies)
    rows = (normed * gain_rows(gains)[0]).astype(BF)
    project(rows, wqkv[...], cosine, sine, query_ref, kv_ref.at[:SPAN])


def mix_kernel(*refs):
    kv_refs, refs = refs[:PIECES], refs[PIECES:]
    query_ref, runs_ref, tri_ref, mixed_ref, logs_ref, bias_ref = refs
    keys = jnp.concatenate(
        [
            piece[k * MARKED + SPAN : (k + 1) * MARKED].astype(F32)[:2]
            for piece in kv_refs
            for k in range(PER_PIECE)
        ],
        0,
    )
    order = lax.broadcasted_iota(jnp.int32, (RUNS, ROWS), 0)
    bias = jnp.where((keys < runs_ref[...]) & (order > 1), 0.0, NEG).astype(BF)
    bias_ref[...] = bias
    mixed, logs = attend(query_ref, kv_refs, bias, tri_ref[...])
    for g in range(KV_HEADS):
        mixed_ref[g] = mixed[g]
        logs_ref[g : g + 1] = logs[g]


def first_kernel(*refs):
    (x_ref, mixed_ref, cos_ref, sin_ref), refs = refs[:4], refs[4:]
    a, b, refs = refs[:7], refs[7:14], refs[14:]
    (act_ref, middle_ref, query1_ref, kv1_ref), refs = refs[:4], refs[4:]
    a_scr, a0_scr, b_scr = refs[:3], refs[3:6], refs[6:]
    copies_b = fetch_b(0, b, *b_scr)
    copies_a0 = fetch_a(0, a, *a0_scr)
    copies_a = fetch_a(1, a, *a_scr)
    hidden = read_turned(x_ref)
    flat = ungroup([mixed_ref[g].astype(F32) for g in range(KV_HEADS)]).T.astype(BF)
    wait_all(copies_b + copies_a0 + copies_a)
    w_gate, w_up, w_down, w_out = b_values(b_scr[0])
    middle = hidden + nn(flat, w_out)
    middle_ref[...] = middle
    _, _, _, gate, upper = feed(middle, gain_rows(a0_scr[1])[1], w_gate, w_up)
    inner = (jax.nn.silu(gate) * upper).astype(BF)
    act = (middle + down(inner, w_down)).astype(BF)
    act_ref[...] = act.astype(F32).T.astype(BF)
    _, _, rows = attn_rows(act.astype(F32), gain_rows(a_scr[1])[0])
    project(rows, a_scr[0][...], cos_ref[...], sin_ref[...], query1_ref, kv1_ref)


LANES = 384
CHUNKS = 32


def on_the_way(chunk):
    y, x, core = here()
    to_y, to_x, to_core = chunk // 8, chunk // 2 % 4, chunk % 2
    back_y, back_x = lax.rem(y + 4 - to_y, 4), lax.rem(x + 4 - to_x, 4)
    at = back_x * 4 + back_y if to_core == 0 else back_y * 4 + back_x
    return at, core == to_core


def put_chunk(mine_ref, theirs_ref, chunk, value):
    at, stays = on_the_way(chunk)

    @pl.when(stays)
    def _():
        mine_ref[at] = value

    @pl.when(jnp.logical_not(stays))
    def _():
        theirs_ref[at] = value


def send_chunk(held, mine_ref, theirs_ref, sems, chunk):
    at, stays = on_the_way(chunk)
    mine = pltpu.make_async_copy(held.at[chunk], mine_ref.at[at], sems.at[chunk])
    theirs = pltpu.make_async_copy(held.at[chunk], theirs_ref.at[at], sems.at[chunk])

    @pl.when(stays)
    def _():
        mine.start()

    @pl.when(jnp.logical_not(stays))
    def _():
        theirs.start()

    return mine


def feed_grads(flat, back_refs, mine_ref, theirs_ref, held, sems):
    rows_ref, inner_ref, dgate_ref, dup_ref, df_ref, da_ref = back_refs
    rows = rows_ref[...].astype(F32).T.astype(BF)
    flat = flat.astype(F32).T.astype(BF)
    df = df_ref[...].astype(F32).T.astype(BF)
    copies = []

    def sent(j):
        for r in range(2):
            copies.append(send_chunk(held, mine_ref, theirs_ref, sems, r * 16 + j))

    def put(value, j):
        for half in range(2):
            for r in range(2):
                at = half * HALF + r * QUARTER
                held[r * 16 + j, half] = value[at : at + QUARTER].astype(BF)
        sent(j)

    empty = jnp.zeros((QUARTER, LANES), BF)
    for j in (14, 15):
        for half in range(2):
            for r in range(2):
                held[r * 16 + j, half] = empty
        sent(j)
    for j in range(4):
        lanes = slice(j * LANES, (j + 1) * LANES)
        put(nn(rows, dgate_ref[:, lanes]), j)
        put(nn(rows, dup_ref[:, lanes]), 4 + j)
    for j in range(2):
        for half in range(2):
            at = half * (FF // 2) + j * LANES
            value = nn(df, inner_ref[:, at : at + LANES])
            for top in range(2):
                for r in range(2):
                    line = top * HALF + r * QUARTER
                    held[r * 16 + 8 + 2 * top + j, half] = value[line : line + QUARTER].astype(BF)
        sent(8 + j)
        sent(10 + j)
    put(nn(flat, da_ref[:, :LANES]), 12)
    put(nn(flat, da_ref[:, LANES:]), 13)
    return copies


def second_kernel(*refs):
    kv_refs, refs = refs[:PIECES], refs[PIECES:]
    (x_ref, cot_ref, query_ref, bias_ref, tri_ref, cos_ref, sin_ref), refs = refs[:7], refs[7:]
    a, b, refs = refs[:7], refs[7:14], refs[14:]
    (act_ref, dh2_ref, dq_ref, gain_ref), refs = refs[:4], refs[4:]
    dkv_refs, grads_refs, refs = refs[:PIECES], refs[PIECES : PIECES + 2], refs[PIECES + 2 :]
    a_scr, b_scr, back_refs, held = refs[:3], refs[3:5], refs[5:11], refs[11:]
    copies_b = fetch_b(1, b, *b_scr)
    copies_a = fetch_a(1, a, *a_scr)
    bias, triangle = bias_ref[...], tri_ref[...]
    mixed, logs = attend(query_ref, kv_refs, bias, triangle)
    wait_all(copies_b + copies_a)
    w_gate, w_up, w_down, w_out = b_values(b_scr[0])
    flat = ungroup([m.astype(F32) for m in mixed]).T.astype(BF)
    middle = read_turned(x_ref) + nn(flat, w_out)
    gain = gain_rows(a_scr[1])[1]
    parts = feed(middle, gain, w_gate, w_up)
    dh2, do = feed_back(
        read_turned(cot_ref), middle, gain, w_gate, w_up, w_down, w_out, parts, (*back_refs, gain_ref)
    )
    copies = feed_grads(flat, back_refs, *grads_refs, *held)
    act_ref[...] = (middle + down(back_refs[1][...], w_down)).T.astype(BF)
    dh2_ref[...] = dh2
    dq = attend_back(query_ref, kv_refs, bias, triangle, mixed, logs, do, dkv_refs)
    dq_ref[...] = query_back(dq, cos_ref[...], sin_ref[...])
    wait_all(copies)


def third_kernel(*refs):
    kv_refs, refs = refs[:PIECES], refs[PIECES:]
    own_dkv, refs = refs[:4], refs[4:]
    (act_ref, dh2_ref, dq_ref, mixed_ref, logs_ref, middle_ref, query_ref), refs = refs[:7], refs[7:]
    (bias_ref, tri_ref, cos_ref, sin_ref), refs = refs[:4], refs[4:]
    a, b, refs = refs[:7], refs[7:14], refs[14:]
    (grad1_ref, rows1_ref, dqkv1_ref, gain1_ref), refs = refs[:4], refs[4:]
    (dh2_out_ref, dq_out_ref, gain_ref), refs = refs[:3], refs[3:]
    dkv_refs, grads_refs, refs = refs[:PIECES], refs[PIECES : PIECES + 2], refs[PIECES + 2 :]
    a_scr, a0_scr, b_scr, back_refs, held = refs[:3], refs[3:6], refs[6:8], refs[8:14], refs[14:]
    copies_a = fetch_a(1, a, *a_scr)
    copies_a0 = fetch_a(0, a, *a0_scr)
    copies_b = fetch_b(0, b, *b_scr)
    cosine, sine = cos_ref[...], sin_ref[...]
    wait_all(copies_a)
    grad = entry_back(
        read_turned(act_ref), gain_rows(a_scr[1])[0], a_scr[0][...], cosine, sine,
        dq_ref[...], own_dkv, dh2_ref[...], rows1_ref, dqkv1_ref, gain1_ref,
    )
    grad1_ref[...] = grad.T
    wait_all(copies_a0 + copies_b)
    w_gate, w_up, w_down, w_out = b_values(b_scr[0])
    mixed = [mixed_ref[g] for g in range(KV_HEADS)]
    logs = [logs_ref[g : g + 1] for g in range(KV_HEADS)]
    flat = ungroup([m.astype(F32) for m in mixed]).T.astype(BF)
    gain = gain_rows(a0_scr[1])[1]
    middle = middle_ref[...]
    parts = feed(middle, gain, w_gate, w_up)
    dh2, do = feed_back(
        grad.astype(BF).astype(F32), middle, gain, w_gate, w_up, w_down, w_out, parts, (*back_refs, gain_ref)
    )
    copies_g = feed_grads(flat, back_refs, *grads_refs, *held)
    dh2_out_ref[...] = dh2
    dq = attend_back(query_ref, kv_refs, bias_ref[...], tri_ref[...], mixed, logs, do, dkv_refs)
    dq_out_ref[...] = query_back(dq, cosine, sine)
    wait_all(copies_g)


def close_kernel(*refs):
    own_dkv, refs = refs[:4], refs[4:]
    (x_ref, dh2_ref, dq_ref, cos_ref, sin_ref), refs = refs[:5], refs[5:]
    a, refs = refs[:7], refs[7:]
    (grad_ref, rows_ref, dqkv_ref, gain_ref), a_scr = refs[:4], refs[4:]
    copies = fetch_a(0, a, *a_scr)
    wait_all(copies)
    grad = entry_back(
        read_turned(x_ref), gain_rows(a_scr[1])[0], a_scr[0][...], cos_ref[...], sin_ref[...],
        dq_ref[...], own_dkv, dh2_ref[...], rows_ref, dqkv_ref, gain_ref,
    )
    grad_ref[...] = grad.T


def entry_grads_kernel(*refs):
    mine_ref, theirs_ref = refs[8:]
    values = []
    for layer in range(2):
        rows_ref, dqkv_ref, gain_attn_ref, gain_mlp_ref = refs[4 * layer : 4 * layer + 4]
        rows = rows_ref[...].astype(F32).T.astype(BF)
        value = nn(rows, dqkv_ref[...])
        gains = jnp.concatenate(
            [gain_attn_ref[...], gain_mlp_ref[...], jnp.zeros((HEAD_DIM - 2, D), F32)], 0
        ).T
        values.append(jnp.concatenate([value, gains], 1).astype(BF))
    for r in range(2):
        for j in range(16):
            lanes = slice(j * HEAD_DIM, (j + 1) * HEAD_DIM)
            parts = [
                value[half * HALF + r * QUARTER : half * HALF + (r + 1) * QUARTER, lanes]
                for value in values
                for half in range(2)
            ]
            put_chunk(mine_ref, theirs_ref, r * 16 + j, jnp.concatenate(parts, 1))


def merge_kernel(*refs):
    feeds, entries, early, merged = refs[:4], refs[4:8], refs[8:12], refs[12:]
    for k in range(4):
        feed0 = sum(part[k].astype(F32) for part in feeds)
        entry = sum(part[k].astype(F32) for part in entries)
        for layer in range(2):
            for half in range(2):
                at = 2 * layer + half
                block = feed0[half].astype(BF) if layer == 0 else early[k][half]
                merged[k][at, :, :LANES] = block
                merged[k][at, :, LANES:] = entry[:, at * HEAD_DIM : (at + 1) * HEAD_DIM].astype(BF)


def unpack_kernel(*refs):
    came, refs = refs[:8], refs[8:]
    (norms_ref, query_ref, key_ref, value_ref, out_ref, gate_ref, up_ref, down_ref), (held,) = refs[:8], refs[8:]
    y, x, core = here()
    for piece in range(8):
        which = core if piece < 4 else 1 - core
        k2 = piece % 4
        for k1 in range(4):
            back_y = jnp.where(which == 0, k1, k2)
            back_x = jnp.where(which == 0, k2, k1)
            chunk = lax.rem(y + 4 - back_y, 4) * 8 + lax.rem(x + 4 - back_x, 4) * 2 + which
            held[chunk] = came[piece][k1]
    for r in range(2):
        rows = slice(r * QUARTER, (r + 1) * QUARTER)

        def block(j):
            return held[r * 16 + j, :, :LANES].astype(F32)

        def head(j):
            return held[r * 16 + j, :, LANES:].astype(F32)

        for j in range(4):
            lanes = slice(j * LANES, (j + 1) * LANES)
            gate_ref[rows, lanes] = block(j)
            up_ref[rows, lanes] = block(4 + j)
        for j in range(2):
            lanes = slice(j * LANES, (j + 1) * LANES)
            for top in range(2):
                down_ref[top * HALF + r * QUARTER : top * HALF + (r + 1) * QUARTER, lanes] = block(8 + 2 * top + j)
        out_ref[rows] = jnp.concatenate([block(12), block(13)[:, : D - LANES]], 1)
        query_ref[rows] = jnp.concatenate([head(j) for j in range(HEADS)], 1)
        key_ref[rows] = jnp.concatenate([head(HEADS + j) for j in range(KV_HEADS)], 1)
        value_ref[rows] = jnp.concatenate([head(HEADS + KV_HEADS + j) for j in range(KV_HEADS)], 1)
    turned = jnp.concatenate([held[r * 16 + 15, :, LANES:].astype(F32).T for r in range(2)], 1)
    norms_ref[...] = turned[:8]


def routes(axes_size):
    def turn_of(i, along_y, k):
        core, x, y = i % 2, i // 2 % 4, i // 8
        if along_y:
            y = (y + k) % 4
        else:
            x = (x + k) % 4
        return y * 8 + x * 2 + core

    def first(k):
        return [(i, turn_of(i, i % 2 == 0, k)) for i in range(axes_size)]

    def second(k):
        return [(i, turn_of(i, i % 2 == 1, k)) for i in range(axes_size)]

    return first, second, [(i, i ^ 1) for i in range(axes_size)]


def per_device(
    inputs, cotangent, positions, norm_attn, w_query, w_key, w_value, w_out, norm_mlp, w_gate, w_up, w_down
):
    section = lax.axis_index("section")
    place = lax.axis_index("ctx")
    core = place % 2
    first, second, swap = routes(lax.axis_size("ctx"))

    def hop(block, route):
        return lax.ppermute(block, "ctx", route)

    def along_z(block, flip):
        return lax.ppermute(block, ("section", "wsh"), [(i, i ^ flip) for i in range(4)])

    spots = lax.dynamic_index_in_dim(positions, section, 0, keepdims=False)[0]
    gains = jnp.concatenate(
        [norm_attn, jnp.zeros((1, 96), BF), norm_mlp, jnp.zeros((1, A_WIDTH - 384 - HALF), BF)], 1
    )
    gains = jnp.concatenate([gains, jnp.zeros((15, A_WIDTH), BF)], 0)
    own_a = jnp.concatenate([w_query[0], w_key[0], w_value[0]], 1)
    half_a = jnp.concatenate([lax.dynamic_slice_in_dim(own_a, core * QUARTER, QUARTER, 0), gains], 0)
    own_a = jnp.concatenate([own_a, gains], 0)
    turned = w_down[0].T
    parts_b = [w_gate[0], w_up[0], turned[:HALF], turned[HALF:], w_out[0]]
    spare = B_WIDTH - OUT_AT - D
    own_b = jnp.concatenate(parts_b + [jnp.zeros((HALF, spare), BF)], 1)
    parts_b = [lax.dynamic_slice_in_dim(part, core * QUARTER, QUARTER, 0) for part in parts_b]
    half_b = jnp.concatenate(parts_b + [jnp.zeros((QUARTER, spare), BF)], 1)

    y, x_at = place // 8, place // 2 % 4
    ring_place = jnp.where(core == 0, y, x_at)
    part = along_z(lax.dynamic_slice_in_dim(half_b, ring_place * B_PART, B_PART, 1), 1)
    came = [along_z(half_a, flip) for flip in (2, 1, 3)]
    a = [own_a] + came + [hop(block, swap) for block in came]

    x = lax.dynamic_index_in_dim(inputs, section, 0, keepdims=False)[0].T
    cot = lax.dynamic_index_in_dim(cotangent, section, 0, keepdims=False)[0].T
    freq = BASE ** (-(jnp.arange(HEAD_DIM // 2, dtype=F32) * 2.0 / HEAD_DIM))
    angle = freq[:, None] * spots.astype(F32)[None, :]
    cosine, sine = jnp.cos(angle), jnp.sin(angle)
    triangle = jnp.where(spots[:, None] <= spots[None, :], 0.0, NEG).astype(F32)

    run_of = spots // RUN
    runs_mine = jnp.concatenate([run_of[:1], run_of[RUN : RUN + 1], jnp.zeros((14,), jnp.int32)])
    runs_mine = jnp.broadcast_to(runs_mine[:, None], (16, KVW)).astype(BF)
    runs_query = jnp.tile(run_of, GROUP).astype(F32)[None]

    def gathered(own):
        four = jnp.concatenate([own] + [hop(own, first(k)) for k in (1, 2, 3)], 0)
        mine = [four] + [hop(four, second(k)) for k in (1, 2, 3)]
        return mine + [hop(piece, swap) for piece in mine]

    def summed(pieces, later=None):
        mine = [add(pieces[k], hop(pieces[4 + k], swap)) for k in range(4)]
        if later is not None:
            later, _ = lax.optimization_barrier((later, mine))
        four = add(mine[0], *[hop(mine[k], second(-k)) for k in (1, 2, 3)])
        parts = [four[k * SPAN : (k + 1) * SPAN] for k in range(4)]
        parts = [parts[0]] + [hop(parts[k], first(-k)) for k in (1, 2, 3)]
        return parts if later is None else (parts, later)

    def add(*parts):
        return sum(part.astype(F32) for part in parts).astype(BF)

    half_b, *_ = lax.optimization_barrier((half_b, *came))
    near, across = along_z(half_b, 2), along_z(half_b, 3)
    query0, own0 = call(
        open_kernel, [(VM, [x, cosine, sine, runs_mine]), (HBM, a)], [QUERY, shape((MARKED, KVW))], A_SCRATCH, 10**8
    )
    all0 = gathered(own0)
    part, *_ = lax.optimization_barrier((part, *all0[1:4]))
    far = [part] + [hop(part, first(k)) for k in (1, 2, 3)]
    mixed0, logs0, bias = call(
        mix_kernel,
        [(VM, all0 + [query0, runs_query, triangle])],
        [MIXED, LOGS, shape((RUNS, ROWS))],
        [],
        10**9,
    )
    mixed0, near, across, *far = lax.optimization_barrier((mixed0, near, across, *far))
    far = jnp.stack(far)
    b = [own_b, near, far, across] + [hop(block, swap) for block in (near, far, across)]
    act0, middle0, query1, own1 = call(
        first_kernel,
        [(VM, [x, mixed0, cosine, sine]), (HBM, a + b)],
        [TURNED, TOKENS32, QUERY, OWN],
        A_SCRATCH + A_SCRATCH + B_SCRATCH,
        10**9,
    )
    all1 = gathered(own1)
    act1, dh2, dq, gain_mlp1, *rest = call(
        second_kernel,
        [(VM, all1 + [act0, cot, query1, bias, triangle, cosine, sine]), (HBM, a + b)],
        [TURNED, TOKENS32, TOKENS, GAIN] + [PIECE] * PIECES + FEEDS,
        A_SCRATCH + B_SCRATCH + GRAD_SCRATCH,
        7 * 10**9,
        2,
    )
    dkv, feed1 = rest[:PIECES], rest[PIECES:]

    def exchanged(own, other):
        kept = jnp.where(section == 0, own, other)
        sent = jnp.where(section == 0, other, own)
        came = lax.ppermute(sent, "section", [(0, 1), (1, 0)])
        return jnp.where(section == 0, jnp.stack([kept, came]), jnp.stack([came, kept]))

    def to_cores(mine, theirs):
        came = hop(theirs, swap)
        return [add(mine[4 * k : 4 * k + 4], came[4 * k : 4 * k + 4]) for k in range(4)]

    def to_rings(sets):
        return [sets[0]] + [hop(sets[k], second(-k)) for k in (1, 2, 3)]

    ENTRIES = [shape((16, QUARTER, 4 * HEAD_DIM))] * 2
    own_dkv = summed(dkv)
    feed1 = to_cores(*feed1)
    acts = exchanged(act0, act1)
    dq, acts, *feed1 = lax.optimization_barrier((dq, acts, *feed1))
    feed1, _ = lax.optimization_barrier((feed1, own_dkv))
    feed1 = to_rings(feed1)
    (
        grad1, rows_in1, dqkv1, gain_attn1,
        dh2, dq, gain_mlp0, *rest,
    ) = call(
        third_kernel,
        [
            (VM, all0 + own_dkv + [act0, dh2, dq, mixed0, logs0, middle0, query0]),
            (VM, [bias, triangle, cosine, sine]),
            (HBM, a + b),
        ],
        [TURNED32, TOKENS, shape((SPAN, QKV)), GAIN]
        + [TOKENS32, TOKENS, GAIN]
        + [PIECE] * PIECES
        + FEEDS,
        A_SCRATCH + A_SCRATCH + B_SCRATCH + GRAD_SCRATCH,
        6 * 10**9,
        2,
    )
    (grad1, rows_in1, dqkv1, gain_attn1, dh2, dq, gain_mlp0, rest, feed1) = lax.optimization_barrier(
        (grad1, rows_in1, dqkv1, gain_attn1, dh2, dq, gain_mlp0, rest, feed1)
    )
    dkv, feed0 = rest[:PIECES], rest[PIECES:]
    own_dkv, feed0[1] = summed(dkv, feed0[1])
    feed0 = to_cores(*feed0)
    early = [add(*[block[k] for block in feed1]) for k in range(4)]
    *own_dkv, feed0, early = lax.optimization_barrier((*own_dkv, feed0, early))
    feed0 = to_rings(feed0)
    grad0, rows_in0, dqkv0, gain_attn0 = call(
        close_kernel,
        [(VM, own_dkv + [x, dh2, dq, cosine, sine]), (HBM, a)],
        [TURNED32, TOKENS, shape((SPAN, QKV)), GAIN],
        A_SCRATCH,
        10**8,
    )
    entries = call(
        entry_grads_kernel,
        [(VM, [rows_in0, dqkv0, gain_attn0, gain_mlp0, rows_in1, dqkv1, gain_attn1, gain_mlp1])],
        ENTRIES,
        [],
        10**8,
    )
    entries, feed0 = lax.optimization_barrier((list(entries), feed0))
    entries = to_rings(to_cores(*entries))
    grads = exchanged(grad0, grad1)
    merged = call(
        merge_kernel, [(VM, feed0 + entries + early)], [shape((4, QUARTER, LANES + HEAD_DIM))] * 4, [], 10**8
    )

    every = add(merged[0], *[hop(merged[k], first(-k)) for k in (1, 2, 3)])
    spot = section * 2 + lax.axis_index("wsh")

    def chunk(flip):
        return lax.dynamic_index_in_dim(every, spot ^ flip, 0, keepdims=False)

    total = add(chunk(0), *[along_z(chunk(flip), flip) for flip in (1, 2, 3)])
    four = jnp.stack([total] + [hop(total, first(k)) for k in (1, 2, 3)])
    mine = [four] + [hop(four, second(k)) for k in (1, 2, 3)]
    mine[1], grads = lax.optimization_barrier((mine[1], grads))
    came = mine + [hop(piece, swap) for piece in mine]
    norms, g_query, g_key, g_value, g_out, g_gate, g_up, g_down = call(
        unpack_kernel,
        [(VM, came)],
        [
            shape((8, HALF), F32), shape((HALF, D), F32), shape((HALF, KVW // 2), F32), shape((HALF, KVW // 2), F32),
            shape((HALF, D), F32), shape((HALF, FF), F32), shape((HALF, FF), F32), shape((D, FF // 2), F32),
        ],
        [pltpu.VMEM((CHUNKS, QUARTER, LANES + HEAD_DIM), BF)],
        10**8,
    )

    return (
        acts.swapaxes(1, 2)[None, :, None],
        grads.swapaxes(1, 2)[None, :, None],
        norms[0:1],
        g_query[None],
        g_key[None],
        g_value[None],
        g_out[None],
        norms[1:2],
        g_gate[None],
        g_up[None],
        g_down.T[None],
    )


def solution(mesh):
    placed = (
        P(None, "wsh", "ctx", None),
        P(None, "wsh", "ctx", None),
        P(None, "wsh", "ctx"),
        P("section", "wsh"),
        P("section", "wsh", None),
        P("section", "wsh", None),
        P("section", "wsh", None),
        P("section", "wsh", None),
        P("section", "wsh"),
        P("section", "wsh", None),
        P("section", "wsh", None),
        P("section", "wsh", None),
    )
    return jax.shard_map(
        per_device,
        mesh=mesh,
        in_specs=placed,
        out_specs=(
            P("section", None, "wsh", "ctx", None),
            P("section", None, "wsh", "ctx", None),
            P("section", "wsh"),
            P("section", "wsh", None),
            P("section", "wsh", None),
            P("section", "wsh", None),
            P("section", "wsh", None),
            P("section", "wsh"),
            P("section", "wsh", None),
            P("section", "wsh", None),
            P("section", "wsh", None),
        ),
        check_vma=False,
    )
```
